256 devices in a mesh: ctx: 32 (over z, x), tp: 8 (over y, core).
Axes of the slice: x: 4, y: 4, z: 8, core: 2. Of those that a mesh axis runs over, the one named last changes fastest.
Arguments:
- tokens: bfloat16 [65536, 4096], P('ctx', 'tp'), may hold values from -6 to 6
- block_counts: int32 [512], P('ctx'), may hold values from 0 to 32, as said below
- block_orders: int32 [512, 128], P('ctx'), may hold values from 0 to 127, each once within a row
- w_router: bfloat16 [4096], P('tp'), may hold values from -0.09375 to 0.09375
- w_query: bfloat16 [4096, 2048], P(None, 'tp'), may hold values from -3 to 3
- w_key: bfloat16 [4096, 1024], P(None, 'tp'), may hold values from -3 to 3
- w_value: bfloat16 [4096, 1024], P(None, 'tp'), may hold values from -0.09375 to 0.09375
- w_out: bfloat16 [2048, 4096], P('tp'), may hold values from -3 to 3
Outputs:
- mixed: bfloat16 [65536, 4096], P('ctx', 'tp')
The draws below stay inside these ranges and needn't reach their ends.
Inputs may be any that keep to these rules, and one draw needn't show every extreme that they name: `block_counts`: the counts of all blocks sum to 8192; the 16 blocks of one index of ctx hold at most 512 routed tokens together, and some index of ctx holds exactly that many.
All inputs are finite; a program needn't handle non-finite values.
Results may differ from the reference program's by a relative error of at most 0.02.
Values may be sent and summed in bfloat16 or wider, within the bound.
A program may use at most 64 MiB of HBM per device.

```python
import math
import jax
import jax.numpy as jnp
from jax import lax

D = 4096
HQ = 16
KVH = 8
HD = 128
TOK_DEV = 2048
TOKENS = 65536
BLOCKS = 512
KEPT = 8192


def shared_keys(key):
    return jax.random.normal(key, (D, KVH * HD), jnp.float32)


def draw_block_counts(key, part):
    key = jax.random.fold_in(key, 11)
    keep = TOK_DEV // 8
    per_shard = TOK_DEV // 128
    shards = BLOCKS // per_shard
    first, second, third = jax.random.split(key, 3)
    order = jax.random.permutation(first, shards)
    moves = jax.random.randint(second, (shards // 2,), 0, keep + 1)
    moves = moves.at[0].set(keep)
    totals = jnp.full((shards,), keep, jnp.int32)
    totals = totals.at[order[0::2]].add(moves).at[order[1::2]].add(-moves)
    base = totals // per_shard
    extra = totals % per_shard
    raw = jax.random.randint(third, (shards, per_shard), 0, 1 << 20)
    scores = raw * per_shard + jnp.arange(per_shard, dtype=jnp.int32)[None, :]
    ranks = jnp.argsort(jnp.argsort(scores, axis=1), axis=1).astype(jnp.int32)
    counts = base[:, None] + (ranks < extra[:, None]).astype(jnp.int32)
    return counts.reshape(-1).astype(jnp.int32)


def draw_w_key(key, part):
    common = shared_keys(key)
    return jnp.clip(common * D ** (-0.5), -3.0, 3.0).astype(jnp.bfloat16)


def draw_w_query(key, part):
    key = jax.random.fold_in(key, 13)
    first = jax.random.fold_in(key, 0)
    fresh = jax.random.normal(first, (D, HQ * HD), jnp.float32)
    matrix = fresh * D ** (-0.5)
    return jnp.clip(matrix, -3.0, 3.0).astype(jnp.bfloat16)


def block_levels(rng, shape, cuts, least, largest):
    loudness, own = 1.0, jax.random.fold_in(rng, 6)
    for dim, shards_of in cuts:
        heights = jnp.exp(jax.random.uniform(jax.random.fold_in(own, dim), (shards_of,), jnp.float32, least / len(cuts), largest / len(cuts)))
        loudness = loudness * jnp.repeat(heights, shape[dim] // shards_of).reshape([-1 if axis == dim else 1 for axis in range(len(shape))])
    return loudness


def noise(own_key, dims, width, bound, pieces=(), held_as=jnp.bfloat16):
    loudness = block_levels(own_key, dims, pieces, -0.22, 0.18) if pieces else 1.0
    entries = jax.random.normal(own_key, dims, jnp.float32) * width * loudness
    return jnp.minimum(jnp.maximum(entries, -bound), bound).astype(held_as)


def setup_inputs(seed: int = 0) -> dict:
    streams_of = jax.random.split(jax.random.key(seed), 9)
    tokens = noise(streams_of[0], (TOKENS, D), 1.0, 6.0, ((0, 32), (1, 8)))
    block_counts = draw_block_counts(jax.random.fold_in(streams_of[8], 71), 0)
    block_orders = jax.vmap(lambda own: jax.random.permutation(own, 128))(jax.random.split(streams_of[2], BLOCKS)).reshape((BLOCKS, 128)).astype(jnp.int32)
    w_router = noise(streams_of[3], (D,), D ** -0.5, 0.09375, ((0, 8),))
    w_query = draw_w_query(jax.random.fold_in(streams_of[8], 71), 0)
    w_key = draw_w_key(jax.random.fold_in(streams_of[8], 71), 0)
    w_value = noise(streams_of[6], (D, KVH * HD), D ** -0.5, 0.09375, ((1, 8),))
    w_out = noise(streams_of[7], (HQ * HD, D), 4 ** -0.5, 3.0, ((0, 8),))
    return dict(tokens=tokens, block_counts=block_counts, block_orders=block_orders, w_router=w_router, w_query=w_query, w_key=w_key, w_value=w_value, w_out=w_out)


def reference(tokens, block_counts, block_orders, w_router, w_query, w_key, w_value, w_out):
    blocks = block_counts.shape[0]
    slot_ids = jnp.broadcast_to(jnp.arange(128, dtype=jnp.int32), (blocks, 128))
    inverse = jnp.zeros((blocks, 128), jnp.int32).at[jnp.arange(blocks, dtype=jnp.int32)[:, None], block_orders].set(slot_ids)
    chosen = (inverse < block_counts[:, None]).reshape(-1)
    positions = jnp.nonzero(chosen, size=KEPT)[0].astype(jnp.int32)
    rows = tokens[positions]
    wide = rows.astype(jnp.float32)
    inv = lax.rsqrt(lax.optimization_barrier(jnp.mean(wide * wide, axis=1)) + 1e-05)
    gate = jax.nn.sigmoid(jnp.dot(rows, w_router, preferred_element_type=jnp.float32))
    query = (jnp.dot(rows, w_query, preferred_element_type=jnp.float32) * inv[:, None]).astype(jnp.bfloat16)
    keys = (jnp.dot(rows, w_key, preferred_element_type=jnp.float32) * inv[:, None]).astype(jnp.bfloat16)
    values = (jnp.dot(rows, w_value, preferred_element_type=jnp.float32) * inv[:, None]).astype(jnp.bfloat16)
    group = HQ // KVH
    qblock = math.gcd(KEPT, 256)
    query_blocks = query.reshape(KEPT // qblock, qblock, KVH, group, HD)
    pos_blocks = positions.reshape(KEPT // qblock, qblock)
    key_wide = keys.reshape(KEPT, KVH, HD).astype(jnp.float32)
    value_wide = values.reshape(KEPT, KVH, HD).astype(jnp.float32)

    def attend(item):
        qpart, qpos = item
        scores = jnp.einsum('nkgd,mkd->nkgm', qpart.astype(jnp.float32), key_wide) * HD ** (-0.5)
        allowed = positions[None, None, None, :] <= qpos[:, None, None, None]
        scores = jnp.where(allowed, scores, -1e+30)
        top = lax.optimization_barrier(jnp.max(scores, axis=-1, keepdims=True))
        expo = jnp.where(allowed, jnp.exp(scores - top), 0.0)
        weights = expo.astype(jnp.bfloat16)
        summed = jnp.einsum('nkgm,mkd->nkgd', weights.astype(jnp.float32), value_wide)
        return (summed / lax.optimization_barrier(jnp.sum(expo, axis=-1))[..., None]).astype(jnp.bfloat16)
    attn = lax.map(attend, (query_blocks, pos_blocks)).reshape(KEPT, HQ * HD)
    update = (jnp.dot(attn, w_out, preferred_element_type=jnp.float32) * gate[:, None]).astype(jnp.bfloat16)
    new_rows = (wide + update.astype(jnp.float32)).astype(jnp.bfloat16)
    return tokens.at[positions].set(new_rows)
```

```python
import functools
import math

import jax
import jax.numpy as jnp
from jax import lax
from jax.experimental import pallas as pl
from jax.experimental.pallas import tpu as pltpu
from jax.sharding import PartitionSpec as P

NX, NY, NZ = 4, 4, 8
TP = 2 * NY
SLOTS = 512
PICK = 32
HEAD = 16
EXT = HEAD + SLOTS
HD = 128
PARTS = 2
ROWS = SLOTS // PARTS
SCALE = HD ** (-0.5) * math.log2(math.e)
MESH = pl.DeviceIdType.MESH
F32, BF16 = jnp.float32, jnp.bfloat16
VMEM = pl.BlockSpec(memory_space=pltpu.VMEM)
ANY = pl.BlockSpec(memory_space=pl.ANY)
LIMIT = 48 << 20


def span(part):
    if part == 0:
        return 0, HEAD + ROWS
    return HEAD + part * ROWS, ROWS


def halves(start, size):
    first = (size // 2 + 15) // 16 * 16
    return (start, first), (start + first, size - first)


def remote(src, dst, sems, item, device):
    return pltpu.make_async_remote_copy(
        src_ref=src, dst_ref=dst, send_sem=sems[0].at[item], recv_sem=sems[1].at[item],
        device_id=device, device_id_type=MESH,
    )


def greet(partners):
    barrier = pltpu.get_barrier_semaphore()
    for device in partners:
        pl.semaphore_signal(barrier, inc=1, device_id=device, device_id_type=MESH)
    pl.semaphore_wait(barrier, len(partners))


def route_kernel(counts, tokens, orders, router, rows, rank, count, pick):
    blocks = orders.shape[0]
    turned = jnp.transpose(orders[...].astype(F32))
    lane = lax.broadcasted_iota(jnp.int32, (PICK, 128), 1).astype(F32)
    slot = lax.broadcasted_iota(jnp.int32, (PICK, 128), 0)
    chosen = []
    for b in range(blocks):
        hit = (turned[:PICK, b : b + 1] == lane) & (slot < counts[b])
        chosen.append(jnp.sum(jnp.where(hit, 1.0, 0.0), axis=0, keepdims=True))
    upper = (
        lax.broadcasted_iota(jnp.int32, (128, 128), 0) < lax.broadcasted_iota(jnp.int32, (128, 128), 1)
    )
    chosen = jnp.concatenate(chosen, axis=0)
    within = jnp.dot(
        chosen.astype(BF16), jnp.where(upper, 1.0, 0.0).astype(BF16), preferred_element_type=F32
    )
    before = jnp.int32(0)
    index = lax.broadcasted_iota(jnp.int32, (SLOTS, 128), 0).astype(F32)
    for b in range(blocks):
        line = jnp.where(
            chosen[b : b + 1] > 0.5, within[b : b + 1] + before.astype(F32), -1.0
        )
        rank[b : b + 1, :] = line
        pick[:, b * 128 : (b + 1) * 128] = jnp.where(index == line, 1.0, 0.0).astype(BF16)
        before = before + counts[b]
    rows[:HEAD, :] = jnp.broadcast_to(router[...], (HEAD, rows.shape[1]))
    rows[HEAD:, :] = jnp.dot(pick[...], tokens[...], preferred_element_type=F32).astype(BF16)
    high = before // 16
    count[:, :128] = jnp.full((HEAD, 128), high.astype(F32), F32).astype(BF16)
    count[:, 128:] = jnp.full((HEAD, 128), (before - high * 16).astype(F32), F32).astype(BF16)


def route(tokens, counts, orders, router):
    blocks = orders.shape[0]
    columns = tokens.shape[1]
    return pl.pallas_call(
        route_kernel,
        out_shape=(
            jax.ShapeDtypeStruct((EXT, columns), BF16),
            jax.ShapeDtypeStruct((blocks, 128), F32),
            jax.ShapeDtypeStruct((HEAD, 256), BF16),
        ),
        in_specs=[pl.BlockSpec(memory_space=pltpu.SMEM), VMEM, VMEM, VMEM],
        out_specs=(VMEM, VMEM, VMEM),
        scratch_shapes=[pltpu.VMEM((SLOTS, tokens.shape[0]), BF16)],
        compiler_params=pltpu.CompilerParams(vmem_limit_bytes=LIMIT),
        cost_estimate=pl.CostEstimate(flops=1 << 30, bytes_accessed=3 << 20, transcendentals=0),
        name="route",
    )(counts, tokens, orders, router)


class TpGather:
    def __init__(self, own, held, sems, spans):
        tp, ctx = lax.axis_index("tp"), lax.axis_index("ctx")
        y, core = tp // 2, tp % 2
        self.own, self.held, self.sems, self.spans, self.tp = own, held, sems, spans, tp
        self.up_slot = ((y + 1) % NY) * 2 + core
        self.down_slot = ((y + NY - 1) % NY) * 2 + core
        self.far_slot = ((y + 2) % NY) * 2 + core
        self.up, self.down = (ctx, self.up_slot), (ctx, self.down_slot)
        self.sibling = (ctx, y * 2 + 1 - core)
        self.partners = [self.up, self.down, self.sibling]
        self.copies = {}

    def send(self, part, item, src, slot, rows, device):
        copy = remote(
            src.at[pl.ds(*rows)], self.held.at[slot, pl.ds(*rows)], self.sems, part * 9 + item, device
        )
        copy.start()
        self.copies[part, item] = copy

    def begin(self, part):
        rows = self.spans[part]
        self.send(part, 0, self.own, self.tp, rows, self.up)
        self.send(part, 1, self.own, self.tp, rows, self.down)
        self.send(part, 2, self.own, self.tp, rows, self.sibling)

    def middle(self, part):
        rows = self.spans[part]
        low, high = halves(*rows)
        self.copies[part, 0].wait_recv()
        self.send(part, 3, self.held.at[self.down_slot], self.down_slot, low, self.up)
        self.send(part, 5, self.held.at[self.down_slot], self.down_slot, rows, self.sibling)
        self.copies[part, 1].wait_recv()
        self.send(part, 4, self.held.at[self.up_slot], self.up_slot, high, self.down)
        self.send(part, 6, self.held.at[self.up_slot], self.up_slot, rows, self.sibling)

    def end(self, part):
        low, high = halves(*self.spans[part])
        self.copies[part, 3].wait_recv()
        self.send(part, 7, self.held.at[self.far_slot], self.far_slot, low, self.sibling)
        self.copies[part, 4].wait_recv()
        self.send(part, 8, self.held.at[self.far_slot], self.far_slot, high, self.sibling)
        for item in (2, 5, 6, 7, 8):
            self.copies[part, item].wait_recv()

    def drain(self):
        for copy in self.copies.values():
            copy.wait_send()


class RingGather:
    def __init__(self, held, sems, spans, me, size, device_of):
        self.held, self.sems, self.spans, self.me, self.size = held, sems, spans, me, size
        self.up, self.down = device_of((me + 1) % size), device_of((me + size - 1) % size)
        self.partners = [self.up, self.down]
        self.copies = {}

    def send(self, part, hop, way, slot, rows):
        item = hop * 2 + way
        at = self.held.at[slot, pl.ds(*rows)]
        copy = remote(at, at, self.sems, part * self.size + item, self.down if way else self.up)
        copy.start()
        self.copies[part, item] = copy

    def begin(self, part):
        self.send(part, 0, 0, self.me, self.spans[part])
        self.send(part, 0, 1, self.me, self.spans[part])

    def hop(self, part, hop):
        rows = self.spans[part]
        low, high = halves(*rows)
        last = hop == self.size // 2 - 1
        self.copies[part, hop * 2 - 2].wait_recv()
        self.send(part, hop, 0, (self.me + self.size - hop) % self.size, low if last else rows)
        self.copies[part, hop * 2 - 1].wait_recv()
        self.send(part, hop, 1, (self.me + hop) % self.size, high if last else rows)

    def end(self, part):
        self.copies[part, self.size - 2].wait_recv()
        self.copies[part, self.size - 1].wait_recv()

    def drain(self):
        for copy in self.copies.values():
            copy.wait_send()


class Swap:
    def __init__(self, matrix, held, relay, sems):
        tp, ctx = lax.axis_index("tp"), lax.axis_index("ctx")
        self.y, self.core, self.tp, self.ctx = tp // 2, tp % 2, tp, ctx
        self.matrix, self.held, self.relay, self.sems = matrix, held, relay, sems
        self.depth, self.width = held.shape[1], held.shape[2]
        self.copies = {}
        self.cores = [self.core, 1 - self.core]
        self.partners = [self.device(step, core) for step in (1, NY - 1) for core in self.cores]
        self.partners.append((ctx, self.y * 2 + 1 - self.core))

    def slot(self, step, core):
        return ((self.y + step) % NY) * 2 + core

    def device(self, step, core):
        return (self.ctx, self.slot(step, core))

    def block(self, slot, rows):
        return self.matrix.at[pl.ds(*rows), pl.ds(pl.multiple_of(slot * self.width, 512), self.width)]

    def send(self, item, src, dst, device):
        copy = remote(src, dst, self.sems, item, device)
        copy.start()
        self.copies[item] = copy

    def begin(self):
        whole, half = (0, self.depth), self.depth // 2
        sibling = self.y * 2 + 1 - self.core
        for way, step in enumerate((1, NY - 1)):
            for i, core in enumerate(self.cores):
                far = self.slot(2, core)
                self.send(
                    way * 2 + i, self.block(far, (way * half, half)), self.relay.at[way, i],
                    self.device(step, self.core),
                )
        for way, step in enumerate((1, NY - 1)):
            for i, core in enumerate(self.cores):
                self.send(
                    4 + way * 2 + i, self.block(self.slot(step, core), whole), self.held.at[self.tp],
                    self.device(step, core),
                )
        self.send(12, self.block(sibling, whole), self.held.at[self.tp], (self.ctx, sibling))

    def middle(self):
        half = self.depth // 2
        for way, step in enumerate((1, NY - 1)):
            source = self.slot(NY - step, self.core)
            for i, core in enumerate(self.cores):
                self.copies[way * 2 + i].wait_recv()
                self.send(
                    8 + way * 2 + i, self.relay.at[way, i],
                    self.held.at[source, pl.ds(way * half, half)], self.device(step, core),
                )

    def end(self):
        for item in range(4, 13):
            self.copies[item].wait_recv()
        for copy in self.copies.values():
            copy.wait_send()


def project_kernel(
    rows, count, w_query, w_key, w_value, w_out,
    query, pair, gate, columns,
    held, weights, total, square, score, relay,
    a_send, a_recv, z_send, z_recv, x_send, x_recv, w_send, w_recv, local_sem,
):
    ctx, tp = lax.axis_index("ctx"), lax.axis_index("tp")
    z, x = ctx // NX, ctx % NX
    spans = [span(part) for part in range(PARTS)]
    tall = TpGather(rows, held, (a_send, a_recv), spans)
    pairs = RingGather(pair, (z_send, z_recv), spans, z, NZ, lambda at: (at * NX + x, tp))
    queries = RingGather(query, (x_send, x_recv), spans, x, NX, lambda at: (z * NX + at, tp))
    swap = Swap(w_out, columns, relay, (w_send, w_recv))
    width = columns.shape[2]
    inner = weights.shape[0] // TP

    loads = [
        pltpu.make_async_copy(w_query, weights.at[:, pl.ds(0, 256)], local_sem.at[0]),
        pltpu.make_async_copy(w_key, weights.at[:, pl.ds(256, 128)], local_sem.at[1]),
        pltpu.make_async_copy(w_value, weights.at[:, pl.ds(384, 128)], local_sem.at[2]),
        pltpu.make_async_copy(
            w_out.at[:, pl.ds(pl.multiple_of(tp * width, 512), width)], columns.at[tp], local_sem.at[3]
        ),
        pltpu.make_async_copy(rows, held.at[tp], local_sem.at[4]),
    ]
    for load in loads:
        load.start()
    greet(pairs.partners + queries.partners + swap.partners)

    query[x, :HEAD, :] = count[...]
    pair[z, :HEAD, :] = count[...]

    def project(part):
        start = HEAD + part * ROWS
        total[...] = jnp.zeros_like(total)
        square[...] = jnp.zeros_like(square)
        score[...] = jnp.zeros_like(score)

        @pl.loop(0, TP)
        def _(slot):
            block = held[slot, start : start + ROWS, :]
            depth = pl.ds(pl.multiple_of(slot * inner, 512), inner)
            total[...] += jnp.dot(block, weights[depth, :], preferred_element_type=F32)
            router = held[slot, 0:HEAD, :].astype(F32)[0:1]
            wide = block.astype(F32)
            both, dots = wide * wide, wide * router
            square[...] += sum(both[:, c : c + 128] for c in range(0, inner, 128))
            score[...] += sum(dots[:, c : c + 128] for c in range(0, inner, 128))

        inv = lax.rsqrt(jnp.sum(square[...], axis=1, keepdims=True) / weights.shape[0] + 1e-05)
        open_ = jax.nn.sigmoid(jnp.sum(score[...], axis=1, keepdims=True))
        gate[part * ROWS : (part + 1) * ROWS, :] = jnp.broadcast_to(open_, (ROWS, 128))
        query[x, start : start + ROWS, :] = (total[:, :256] * inv).astype(BF16)
        pair[z, start : start + ROWS, :] = (total[:, 256:] * inv).astype(BF16)

    tall.begin(0)
    tall.begin(1)
    tall.middle(0)
    tall.end(0)
    for load in loads:
        load.wait()
    project(0)
    pairs.begin(0)
    queries.begin(0)
    tall.middle(1)
    queries.hop(0, 1)
    pairs.hop(0, 1)
    tall.end(1)
    swap.begin()
    pairs.hop(0, 2)
    project(1)
    pairs.begin(1)
    queries.begin(1)
    pairs.hop(0, 3)
    pairs.hop(1, 1)
    queries.hop(1, 1)
    swap.middle()
    pairs.hop(1, 2)
    pairs.hop(1, 3)
    for part in range(PARTS):
        queries.end(part)
        pairs.end(part)
    swap.end()
    tall.drain()
    queries.drain()
    pairs.drain()


def project(rows, count, w_query, w_key, w_value, w_out):
    width = rows.shape[1]
    deep = w_query.shape[0]
    dma = pltpu.SemaphoreType.DMA
    return pl.pallas_call(
        project_kernel,
        out_shape=(
            jax.ShapeDtypeStruct((NX, EXT, 256), BF16),
            jax.ShapeDtypeStruct((NZ, EXT, 256), BF16),
            jax.ShapeDtypeStruct((SLOTS, 128), F32),
            jax.ShapeDtypeStruct((TP, w_out.shape[0], width), BF16),
        ),
        in_specs=[VMEM, VMEM, ANY, ANY, ANY, ANY],
        out_specs=(VMEM, VMEM, VMEM, ANY),
        scratch_shapes=[
            pltpu.VMEM((TP, EXT, width), BF16),
            pltpu.VMEM((deep, 512), BF16),
            pltpu.VMEM((ROWS, 512), F32),
            pltpu.VMEM((ROWS, 128), F32),
            pltpu.VMEM((ROWS, 128), F32),
            pltpu.VMEM((2, 2, w_out.shape[0] // 2, width), BF16),
            dma((PARTS * 9,)), dma((PARTS * 9,)),
            dma((PARTS * NZ,)), dma((PARTS * NZ,)),
            dma((PARTS * NX,)), dma((PARTS * NX,)),
            dma((13,)), dma((13,)),
            dma((5,)),
        ],
        compiler_params=pltpu.CompilerParams(
            collective_id=0, has_side_effects=True, vmem_limit_bytes=LIMIT
        ),
        cost_estimate=pl.CostEstimate(flops=2 << 30, bytes_accessed=16 << 20, transcendentals=0),
        name="project",
    )(rows, count, w_query, w_key, w_value, w_out)


KEYS = 512
QROWS = 256


def attend_kernel(query, pair, out, stats, kp, vp, qp, op, sp, top, mass, accum):
    ctx = lax.axis_index("ctx")
    z, x = ctx // NX, ctx % NX

    def number(ref, at):
        head = ref[at, :HEAD, :].astype(F32)
        return (jnp.max(head[:, :128]) * 16.0 + jnp.max(head[:, 128:])).astype(jnp.int32)

    def padded(n):
        return (n + 15) // 16 * 16

    one = jnp.where(lax.broadcasted_iota(jnp.int32, (SLOTS, 128), 1) == 0, 1.0, 0.0).astype(BF16)
    slot = lax.broadcasted_iota(jnp.int32, (SLOTS, 128), 0)
    q_from = []
    used = jnp.int32(0)
    for at in range(NX):
        rows = pl.ds(pl.multiple_of(used, 16), SLOTS)
        for head in range(2):
            qp[head, rows, :128] = query[at, HEAD:, head * 128 : (head + 1) * 128]
            qp[head, rows, 128:] = one
        q_from.append(used)
        used = used + padded(number(query, at))
    q_blocks = (used + QROWS - 1) // QROWS

    def pack(at, place, n):
        rows = pl.ds(pl.multiple_of(place, 16), SLOTS)
        kp[rows, :128] = pair[at, HEAD:, :128]
        kp[rows, 128:] = jnp.where(slot < n, 0.0, -1e30).astype(BF16)
        vp[rows, :] = pair[at, HEAD:, 128:]

    here = number(pair, z)
    pack(z, jnp.int32(0), here)

    def earlier(at, place):
        n = number(pair, at)
        pack(at, place, n)
        return place + padded(n)

    last = lax.fori_loop(0, z, earlier, jnp.int32(SLOTS))
    rows = pl.ds(pl.multiple_of(last, 16), SLOTS)
    kp[rows, :128] = jnp.zeros((SLOTS, 128), BF16)
    kp[rows, 128:] = jnp.full((SLOTS, 128), -1e30, BF16)
    vp[rows, :] = jnp.zeros((SLOTS, 128), BF16)
    k_blocks = (last - SLOTS + KEYS - 1) // KEYS

    op[...] = jnp.zeros_like(op)
    sp[...] = jnp.zeros_like(sp)
    mine = jnp.int32(0)
    for at in range(NX):
        mine = jnp.where(x == at, q_from[at], mine)
    mine_end = mine + padded(here)

    def step(q_rows, k_rows, mask):
        keys, values = kp[k_rows, :], vp[k_rows, :]
        for head in range(2):
            scores = lax.dot_general(
                qp[head, q_rows, :], keys, (((1,), (1,)), ((), ())), preferred_element_type=F32
            ) * SCALE
            if mask is not None:
                scores = jnp.where(mask, scores, -1e30)
            old = top[head]
            new = jnp.maximum(old, jnp.max(scores, axis=1, keepdims=True))
            shrink = jnp.exp2(old - new)
            expo = jnp.exp2(scores - new[:, :1])
            if mask is not None:
                expo = jnp.where(mask, expo, 0.0)
            top[head] = new
            mass[head] = mass[head] * shrink + sum(expo[:, c : c + 128] for c in range(0, KEYS, 128))
            accum[head] = accum[head] * shrink + jnp.dot(
                expo.astype(BF16), values, preferred_element_type=F32
            )

    def q_block(at, carry):
        begin = at * QROWS
        q_rows = pl.ds(pl.multiple_of(begin, QROWS), QROWS)
        top[...] = jnp.full_like(top, -1e30)
        mass[...] = jnp.zeros_like(mass)
        accum[...] = jnp.zeros_like(accum)

        @pl.when(begin + QROWS > mine)
        def _():
            row = begin + lax.broadcasted_iota(jnp.int32, (QROWS, KEYS), 0)
            key = lax.broadcasted_iota(jnp.int32, (QROWS, KEYS), 1)
            mask = ((row >= mine) & (key <= row - mine)) | (row >= mine_end)
            step(q_rows, pl.ds(0, KEYS), mask)

        def k_block(kat, carry):
            step(q_rows, pl.ds(pl.multiple_of(SLOTS + kat * KEYS, KEYS), KEYS), None)
            return carry

        lax.fori_loop(0, k_blocks, k_block, 0)
        lane = lax.broadcasted_iota(jnp.int32, (QROWS, 128), 1)
        kept = jnp.zeros((QROWS, 128), F32)
        for head in range(2):
            whole = jnp.sum(mass[head], axis=1, keepdims=True)
            op[q_rows, head * 128 : (head + 1) * 128] = (
                accum[head] / jnp.maximum(whole, 1e-30)
            ).astype(BF16)
            kept = jnp.where(lane == 2 * head, top[head], kept)
            kept = jnp.where(lane == 2 * head + 1, whole, kept)
        sp[q_rows, :] = kept
        return carry

    lax.fori_loop(0, q_blocks, q_block, 0)
    for at in range(NX):
        rows = pl.ds(pl.multiple_of(q_from[at], 16), SLOTS)
        out[at] = op[rows, :]
        stats[at] = jnp.transpose(sp[rows, :])[:8]


def attend(query, pair):
    packed_q = (NX + 1) * SLOTS
    packed_k = (NZ + 1) * SLOTS
    return pl.pallas_call(
        attend_kernel,
        out_shape=(
            jax.ShapeDtypeStruct((NX, SLOTS, 256), BF16),
            jax.ShapeDtypeStruct((NX, 8, SLOTS), F32),
        ),
        in_specs=[VMEM, VMEM],
        out_specs=(VMEM, VMEM),
        scratch_shapes=[
            pltpu.VMEM((packed_k + KEYS, 256), BF16),
            pltpu.VMEM((packed_k + KEYS, 128), BF16),
            pltpu.VMEM((2, packed_q, 256), BF16),
            pltpu.VMEM((packed_q, 256), BF16),
            pltpu.VMEM((packed_q, 128), F32),
            pltpu.VMEM((2, QROWS, 128), F32),
            pltpu.VMEM((2, QROWS, 128), F32),
            pltpu.VMEM((2, QROWS, 128), F32),
        ],
        compiler_params=pltpu.CompilerParams(vmem_limit_bytes=LIMIT),
        cost_estimate=pl.CostEstimate(flops=4 << 30, bytes_accessed=8 << 20, transcendentals=4 << 20),
        name="attend",
    )(query, pair)


def merge_kernel(
    part_out, stats, gate, columns, update,
    came, came_stats, relay, own, held, weights, total,
    x_send, x_recv, s_send, s_recv, a_send, a_recv, local_sem,
):
    ctx, tp = lax.axis_index("ctx"), lax.axis_index("tp")
    z, x = ctx // NX, ctx % NX
    right, left, far = (x + 1) % NX, (x + NX - 1) % NX, (x + 2) % NX

    def at_x(at):
        return (z * NX + at, tp)

    spans = [(part * ROWS, ROWS) for part in range(PARTS)]
    gather = TpGather(own, held, (a_send, a_recv), spans)
    load = pltpu.make_async_copy(columns, weights, local_sem.at[0])
    load.start()
    greet(gather.partners + [at_x(right), at_x(left), at_x(far)])

    copies = {}

    def send(part, item, src, dst, device):
        copy = remote(src, dst, (x_send, x_recv), part * 6 + item, device)
        copy.start()
        copies[part, item] = copy

    told = []
    for item, to in enumerate((right, left, far)):
        copy = remote(stats.at[to], came_stats.at[x], (s_send, s_recv), item, at_x(to))
        copy.start()
        told.append(copy)

    def begin(part):
        rows = spans[part]
        low, high = halves(*rows)
        send(part, 2, part_out.at[far, pl.ds(*low)], relay.at[part, 0], at_x(right))
        send(part, 3, part_out.at[far, pl.ds(*high)], relay.at[part, 1], at_x(left))
        send(part, 0, part_out.at[right, pl.ds(*rows)], came.at[x, pl.ds(*rows)], at_x(right))
        send(part, 1, part_out.at[left, pl.ds(*rows)], came.at[x, pl.ds(*rows)], at_x(left))

    def middle(part):
        low, high = halves(*spans[part])
        copies[part, 2].wait_recv()
        send(part, 4, relay.at[part, 0], came.at[left, pl.ds(*low)], at_x(right))
        copies[part, 3].wait_recv()
        send(part, 5, relay.at[part, 1], came.at[right, pl.ds(*high)], at_x(left))

    def combine(part):
        for item in (0, 1, 4, 5):
            copies[part, item].wait_recv()
        lo = part * ROWS
        lines = [stats[x, :, lo : lo + ROWS]] + [
            came_stats[at, :, lo : lo + ROWS] for at in (right, left, far)
        ]
        shares = []
        for head in range(2):
            tops = [line[2 * head : 2 * head + 1] for line in lines]
            best = functools.reduce(jnp.maximum, tops)
            mass = [
                line[2 * head + 1 : 2 * head + 2] * jnp.exp2(one - best)
                for line, one in zip(lines, tops)
            ]
            whole = jnp.maximum(sum(mass), 1e-30)
            shares += [one / whole for one in mass]
        turned = jnp.transpose(
            jnp.concatenate(shares + [jnp.zeros((120, ROWS), F32)], axis=0)
        )
        blocks = [part_out[x, lo : lo + ROWS, :]] + [
            came[at, lo : lo + ROWS, :] for at in (right, left, far)
        ]
        for head in range(2):
            mixed = sum(
                block[:, head * 128 : (head + 1) * 128].astype(F32)
                * turned[:, head * 4 + i : head * 4 + i + 1]
                for i, block in enumerate(blocks)
            ).astype(BF16)
            own[lo : lo + ROWS, head * 128 : (head + 1) * 128] = mixed
            held[tp, lo : lo + ROWS, head * 128 : (head + 1) * 128] = mixed

    def finish(part):
        lo = part * ROWS
        total[...] = jnp.zeros_like(total)

        @pl.loop(0, TP)
        def _(slot):
            total[...] += jnp.dot(
                held[slot, lo : lo + ROWS, :], weights[slot], preferred_element_type=F32
            )

        update[lo : lo + ROWS, :] = (total[...] * gate[lo : lo + ROWS, :1]).astype(BF16)

    begin(0)
    begin(1)
    middle(0)
    for copy in told:
        copy.wait_recv()
    combine(0)
    gather.begin(0)
    middle(1)
    gather.middle(0)
    combine(1)
    gather.begin(1)
    gather.end(0)
    load.wait()
    gather.middle(1)
    finish(0)
    gather.end(1)
    finish(1)
    for copy in told + list(copies.values()):
        copy.wait_send()
    gather.drain()


def merge(part_out, stats, gate, columns):
    depth, width = columns.shape[1:]
    dma = pltpu.SemaphoreType.DMA
    return pl.pallas_call(
        merge_kernel,
        out_shape=jax.ShapeDtypeStruct((SLOTS, width), BF16),
        in_specs=[VMEM, VMEM, VMEM, ANY],
        out_specs=VMEM,
        scratch_shapes=[
            pltpu.VMEM((NX, SLOTS, 256), BF16),
            pltpu.VMEM((NX, 8, SLOTS), F32),
            pltpu.VMEM((PARTS, 2, ROWS // 2, 256), BF16),
            pltpu.VMEM((SLOTS, 256), BF16),
            pltpu.VMEM((TP, SLOTS, 256), BF16),
            pltpu.VMEM((TP, depth, width), BF16),
            pltpu.VMEM((ROWS, width), F32),
            dma((PARTS * 6,)), dma((PARTS * 6,)),
            dma((3,)), dma((3,)),
            dma((PARTS * 9,)), dma((PARTS * 9,)),
            dma((1,)),
        ],
        compiler_params=pltpu.CompilerParams(
            collective_id=1, has_side_effects=True, vmem_limit_bytes=LIMIT
        ),
        cost_estimate=pl.CostEstimate(flops=1 << 30, bytes_accessed=8 << 20, transcendentals=0),
        name="merge",
    )(part_out, stats, gate, columns)


def spread_kernel(tokens, rank, update, out):
    turned = jnp.transpose(rank[...])
    slot = lax.broadcasted_iota(jnp.int32, (128, SLOTS), 1).astype(F32)
    for b in range(rank.shape[0]):
        place = jnp.where(turned[:, b : b + 1] == slot, 1.0, 0.0).astype(BF16)
        added = jnp.dot(place, update[...], preferred_element_type=F32)
        rows = slice(b * 128, (b + 1) * 128)
        out[rows, :] = (tokens[rows, :].astype(F32) + added).astype(BF16)


def spread(tokens, rank, update):
    tall, width = tokens.shape
    steps = rank.shape[0] // 8
    return pl.pallas_call(
        spread_kernel,
        out_shape=jax.ShapeDtypeStruct((tall, width), BF16),
        grid=(steps,),
        in_specs=[
            pl.BlockSpec((tall // steps, width), lambda i: (i, 0)),
            pl.BlockSpec((8, 128), lambda i: (i, 0)),
            pl.BlockSpec((SLOTS, width), lambda i: (0, 0)),
        ],
        out_specs=pl.BlockSpec((tall // steps, width), lambda i: (i, 0)),
        compiler_params=pltpu.CompilerParams(vmem_limit_bytes=LIMIT),
        cost_estimate=pl.CostEstimate(flops=1 << 30, bytes_accessed=5 << 20, transcendentals=0),
        name="spread",
    )(tokens, rank, update)


def body(tokens, block_counts, block_orders, w_router, w_query, w_key, w_value, w_out):
    rows, rank, count = route(tokens, block_counts, block_orders, w_router[None, :])
    query, pair, gate, columns = project(rows, count, w_query, w_key, w_value, w_out)
    part_out, stats = attend(query, pair)
    update = merge(part_out, stats, gate, columns)
    return spread(tokens, rank, update)


def solution(mesh):
    return jax.shard_map(
        body,
        mesh=mesh,
        in_specs=(
            P("ctx", "tp"),
            P("ctx"),
            P("ctx", None),
            P("tp"),
            P(None, "tp"),
            P(None, "tp"),
            P(None, "tp"),
            P("tp", None),
        ),
        out_specs=P("ctx", "tp"),
        check_vma=False,
    )
```

```python
import functools

import jax
import jax.numpy as jnp
from jax import lax
from jax.experimental import pallas as pl
from jax.experimental.pallas import tpu as pltpu
from jax.sharding import PartitionSpec as P

NX, NY, NZ = 4, 4, 8
TP = 2 * NY
SLOTS = 512
PICK = 32
HEAD = 16
EXT = HEAD + SLOTS
HD = 128
SLOT_SPANS = [(0, 128), (128, 128), (256, 128), (384, 128)]
SPANS = [(0, HEAD + 128)] + [(HEAD + at, size) for at, size in SLOT_SPANS[1:]]
PARTS = len(SPANS)
LARGEST = 128
MERGES = 2
ROWS = SLOTS // MERGES
DONE = 256
SCALE = HD ** (-0.5)
MESH = pl.DeviceIdType.MESH
F32, BF16 = jnp.float32, jnp.bfloat16
VMEM = pl.BlockSpec(memory_space=pltpu.VMEM)
FAR = pl.BlockSpec(memory_space=pltpu.HBM)
MIB = 1 << 20


def halves(start, size, unit=16):
    first = -(-(size // 2) // unit) * unit
    return (start, first), (start + first, size - first)


def remote(src, dst, sems, item, device):
    return pltpu.make_async_remote_copy(
        src_ref=src, dst_ref=dst, send_sem=sems[0].at[item], recv_sem=sems[1].at[item],
        device_id=device, device_id_type=MESH,
    )


def greet(partners):
    barrier = pltpu.get_barrier_semaphore()
    for device in partners:
        pl.semaphore_signal(barrier, inc=1, device_id=device, device_id_type=MESH)
    pl.semaphore_wait(barrier, len(partners))


def route_kernel(
    far_counts, far_tokens, far_orders, router, rows, rank, count, counts, tokens, orders, pick, total, sems
):
    blocks = orders.shape[0]
    tall = tokens.shape[0] // 4
    small = [
        pltpu.make_async_copy(far_counts, counts, sems.at[0]),
        pltpu.make_async_copy(far_orders, orders, sems.at[1]),
    ]
    large = [
        pltpu.make_async_copy(
            far_tokens.at[pl.ds(at * tall, tall)], tokens.at[pl.ds(at * tall, tall)], sems.at[2 + at]
        )
        for at in range(4)
    ]
    for copy in small + large:
        copy.start()
    for copy in small:
        copy.wait()
    turned = jnp.transpose(orders[...].astype(F32))
    lane = lax.broadcasted_iota(jnp.int32, (PICK, 128), 1).astype(F32)
    slot = lax.broadcasted_iota(jnp.int32, (PICK, 128), 0)
    chosen = []
    for b in range(blocks):
        hit = (turned[:PICK, b : b + 1] == lane) & (slot < counts[b])
        chosen.append(jnp.sum(jnp.where(hit, 1.0, 0.0), axis=0, keepdims=True))
    upper = (
        lax.broadcasted_iota(jnp.int32, (128, 128), 0) < lax.broadcasted_iota(jnp.int32, (128, 128), 1)
    )
    chosen = jnp.concatenate(chosen, axis=0)
    within = jnp.dot(
        chosen.astype(BF16), jnp.where(upper, 1.0, 0.0).astype(BF16), preferred_element_type=F32
    )
    before = jnp.int32(0)
    index = lax.broadcasted_iota(jnp.int32, (SLOTS, 128), 0).astype(F32)
    for b in range(blocks):
        line = jnp.where(
            chosen[b : b + 1] > 0.5, within[b : b + 1] + before.astype(F32), -1.0
        )
        rank[b : b + 1, :] = line
        pick[:, b * 128 : (b + 1) * 128] = jnp.where(index == line, 1.0, 0.0).astype(BF16)
        before = before + counts[b]
    rows[:HEAD, :] = jnp.broadcast_to(router[...].reshape(1, rows.shape[1]), (HEAD, rows.shape[1]))
    for at, copy in enumerate(large):
        copy.wait()
        some = slice(at * tall, (at + 1) * tall)
        made = jnp.dot(pick[:, some], tokens[some, :], preferred_element_type=F32)
        if at == 0:
            total[...] = made
        elif at < 3:
            total[...] += made
        else:
            rows[HEAD:, :] = (total[...] + made).astype(BF16)
    high = before // 16
    count[:, :128] = jnp.full((HEAD, 128), high.astype(F32), F32).astype(BF16)
    count[:, 128:] = jnp.full((HEAD, 128), (before - high * 16).astype(F32), F32).astype(BF16)


def route(tokens, counts, orders, router):
    blocks = orders.shape[0]
    columns = tokens.shape[1]
    return pl.pallas_call(
        route_kernel,
        out_shape=(
            jax.ShapeDtypeStruct((EXT, columns), BF16),
            jax.ShapeDtypeStruct((blocks, 128), F32),
            jax.ShapeDtypeStruct((HEAD, 256), BF16),
        ),
        in_specs=[FAR, FAR, FAR, VMEM],
        out_specs=(VMEM, VMEM, VMEM),
        scratch_shapes=[
            pltpu.SMEM(counts.shape, jnp.int32),
            pltpu.VMEM(tokens.shape, BF16),
            pltpu.VMEM(orders.shape, jnp.int32),
            pltpu.VMEM((SLOTS, tokens.shape[0]), BF16),
            pltpu.VMEM((SLOTS, columns), F32),
            pltpu.SemaphoreType.DMA((6,)),
        ],
        compiler_params=pltpu.CompilerParams(vmem_limit_bytes=12 * MIB),
        cost_estimate=pl.CostEstimate(flops=1 << 30, bytes_accessed=3 << 20, transcendentals=0),
        name="route",
    )(counts, tokens, orders, router)


class TpGather:
    def __init__(self, own, held, sems, spans):
        tp, ctx = lax.axis_index("tp"), lax.axis_index("ctx")
        y, core = tp // 2, tp % 2
        self.own, self.held, self.sems, self.spans, self.tp = own, held, sems, spans, tp
        self.up_slot = ((y + 1) % NY) * 2 + core
        self.down_slot = ((y + NY - 1) % NY) * 2 + core
        self.far_slot = ((y + 2) % NY) * 2 + core
        self.up, self.down = (ctx, self.up_slot), (ctx, self.down_slot)
        self.sibling = (ctx, y * 2 + 1 - core)
        self.partners = [self.up, self.down, self.sibling]
        self.copies = {}

    def send(self, part, item, src, slot, rows, device):
        copy = remote(
            src.at[pl.ds(*rows)], self.held.at[slot, pl.ds(*rows)], self.sems, part * 9 + item, device
        )
        copy.start()
        self.copies[part, item] = copy

    def begin(self, part):
        rows = self.spans[part]
        self.send(part, 0, self.own, self.tp, rows, self.up)
        self.send(part, 1, self.own, self.tp, rows, self.down)
        self.send(part, 2, self.own, self.tp, rows, self.sibling)

    def middle(self, part):
        rows = self.spans[part]
        low, high = halves(*rows)
        self.copies[part, 0].wait_recv()
        self.send(part, 3, self.held.at[self.down_slot], self.down_slot, low, self.up)
        self.send(part, 5, self.held.at[self.down_slot], self.down_slot, rows, self.sibling)
        self.copies[part, 1].wait_recv()
        self.send(part, 4, self.held.at[self.up_slot], self.up_slot, high, self.down)
        self.send(part, 6, self.held.at[self.up_slot], self.up_slot, rows, self.sibling)

    def end(self, part):
        low, high = halves(*self.spans[part])
        self.copies[part, 3].wait_recv()
        self.send(part, 7, self.held.at[self.far_slot], self.far_slot, low, self.sibling)
        self.copies[part, 4].wait_recv()
        self.send(part, 8, self.held.at[self.far_slot], self.far_slot, high, self.sibling)
        for item in (2, 5, 6, 7, 8):
            self.copies[part, item].wait_recv()

    def drain(self):
        for copy in self.copies.values():
            copy.wait_send()


class RingGather:
    def __init__(self, held, sems, spans, me, size, device_of, unit=16):
        self.held, self.sems, self.spans, self.me, self.size = held, sems, spans, me, size
        self.up, self.down = device_of((me + 1) % size), device_of((me + size - 1) % size)
        self.partners = [self.up, self.down]
        self.unit = unit
        self.copies = {}

    def send(self, part, hop, way, slot, rows):
        item = hop * 2 + way
        at = self.held.at[slot, pl.ds(*rows)]
        copy = remote(at, at, self.sems, part * self.size + item, self.down if way else self.up)
        copy.start()
        self.copies[part, item] = copy

    def begin(self, part):
        self.send(part, 0, 0, self.me, self.spans[part])
        self.send(part, 0, 1, self.me, self.spans[part])

    def hop(self, part, hop):
        rows = self.spans[part]
        low, high = halves(*rows, self.unit)
        last = hop == self.size // 2 - 1
        self.copies[part, hop * 2 - 2].wait_recv()
        self.send(part, hop, 0, (self.me + self.size - hop) % self.size, low if last else rows)
        self.copies[part, hop * 2 - 1].wait_recv()
        self.send(part, hop, 1, (self.me + hop) % self.size, high if last else rows)

    def end(self, part):
        self.copies[part, self.size - 2].wait_recv()
        self.copies[part, self.size - 1].wait_recv()

    def drain(self):
        for copy in self.copies.values():
            copy.wait_send()


class Swap:
    def __init__(self, matrix, held, relay, sems, first):
        tp, ctx = lax.axis_index("tp"), lax.axis_index("ctx")
        self.y, self.core, self.tp, self.ctx = tp // 2, tp % 2, tp, ctx
        self.matrix, self.held, self.relay, self.sems = matrix, held, relay, sems
        self.depth, self.width = held.shape[1], held.shape[2]
        self.first = first
        self.copies = {}
        self.cores = [self.core, 1 - self.core]
        self.partners = [self.device(step, core) for step in (1, NY - 1) for core in self.cores]
        self.partners.append((ctx, self.y * 2 + 1 - self.core))

    def slot(self, step, core):
        return ((self.y + step) % NY) * 2 + core

    def device(self, step, core):
        return (self.ctx, self.slot(step, core))

    def block(self, slot, rows):
        start, size = rows
        rows = pl.ds(pl.multiple_of(self.first + start, 16), size)
        return self.matrix.at[rows, pl.ds(pl.multiple_of(slot * self.width, 512), self.width)]

    def send(self, item, src, dst, device):
        copy = remote(src, dst, self.sems, item, device)
        copy.start()
        self.copies[item] = copy

    def begin(self):
        whole, half = (0, self.depth), self.depth // 2
        sibling = self.y * 2 + 1 - self.core
        for way, step in enumerate((1, NY - 1)):
            for i, core in enumerate(self.cores):
                far = self.slot(2, core)
                self.send(
                    way * 2 + i, self.block(far, (way * half, half)), self.relay.at[way, i],
                    self.device(step, self.core),
                )
        for way, step in enumerate((1, NY - 1)):
            for i, core in enumerate(self.cores):
                self.send(
                    4 + way * 2 + i, self.block(self.slot(step, core), whole), self.held.at[self.tp],
                    self.device(step, core),
                )
        self.send(12, self.block(sibling, whole), self.held.at[self.tp], (self.ctx, sibling))

    def middle(self):
        half = self.depth // 2
        for way, step in enumerate((1, NY - 1)):
            source = self.slot(NY - step, self.core)
            for i, core in enumerate(self.cores):
                self.copies[way * 2 + i].wait_recv()
                self.send(
                    8 + way * 2 + i, self.relay.at[way, i],
                    self.held.at[source, pl.ds(way * half, half)], self.device(step, core),
                )

    def end(self):
        for item in range(4, 13):
            self.copies[item].wait_recv()

    def drain(self):
        for copy in self.copies.values():
            copy.wait_send()


def project_kernel(
    rows, count, w_query, w_key, w_value, w_out,
    query, pair, gate, columns,
    held, weights, total, square, score, relay,
    a_send, a_recv, z_send, z_recv, x_send, x_recv, w_send, w_recv, c_send, c_recv, local_sem,
):
    ctx, tp = lax.axis_index("ctx"), lax.axis_index("tp")
    z, x = ctx // NX, ctx % NX
    depth, width = columns.shape[2:]
    inner = weights.shape[0] // TP
    tall = TpGather(rows, held, (a_send, a_recv), SPANS)
    pairs = RingGather(pair, (z_send, z_recv), SPANS, z, NZ, lambda at: (at * NX + x, tp))
    queries = RingGather(query, (x_send, x_recv), SPANS, x, NX, lambda at: (z * NX + at, tp))
    swap = Swap(w_out, columns.at[x], relay, (w_send, w_recv), x * depth)
    shares = RingGather(
        columns, (c_send, c_recv), [(0, TP)], x, NX, lambda at: (z * NX + at, tp), 1
    )

    loads = [
        pltpu.make_async_copy(w_query, weights.at[:, pl.ds(0, 256)], local_sem.at[0]),
        pltpu.make_async_copy(w_key, weights.at[:, pl.ds(256, 128)], local_sem.at[1]),
        pltpu.make_async_copy(w_value, weights.at[:, pl.ds(384, 128)], local_sem.at[2]),
        pltpu.make_async_copy(
            w_out.at[
                pl.ds(pl.multiple_of(x * depth, 16), depth),
                pl.ds(pl.multiple_of(tp * width, 512), width),
            ],
            columns.at[x, tp],
            local_sem.at[3],
        ),
        pltpu.make_async_copy(rows, held.at[tp], local_sem.at[4]),
    ]
    for load in loads:
        load.start()
    greet(pairs.partners + queries.partners + swap.partners)

    def project(part):
        start, size = SLOT_SPANS[part]
        start += HEAD
        here = slice(0, size)
        total[here, :] = jnp.zeros((size, 512), F32)
        square[here, :] = jnp.zeros((size, 128), F32)
        score[here, :] = jnp.zeros((size, 128), F32)

        @pl.loop(0, TP)
        def _(slot):
            block = held[slot, start : start + size, :]
            deep = pl.ds(pl.multiple_of(slot * inner, 512), inner)
            total[here, :] += jnp.dot(block, weights[deep, :], preferred_element_type=F32)
            router = held[slot, 0:HEAD, :].astype(F32)[0:1]
            wide = block.astype(F32)
            both, dots = wide * wide, wide * router
            square[here, :] += sum(both[:, c : c + 128] for c in range(0, inner, 128))
            score[here, :] += sum(dots[:, c : c + 128] for c in range(0, inner, 128))

        inv = lax.rsqrt(jnp.sum(square[here, :], axis=1, keepdims=True) / weights.shape[0] + 1e-05)
        open_ = jax.nn.sigmoid(jnp.sum(score[here, :], axis=1, keepdims=True))
        gate[start - HEAD : start - HEAD + size, :] = jnp.broadcast_to(open_, (size, 128))
        query[x, start : start + size, :] = (total[here, :256] * inv).astype(BF16)
        pair[z, start : start + size, :] = (total[here, 256:] * inv).astype(BF16)
        pairs.begin(part)
        queries.begin(part)

    tall.begin(0)
    tall.begin(1)
    query[x, :HEAD, :] = count[...]
    pair[z, :HEAD, :] = count[...]
    tall.middle(0)
    tall.begin(2)
    tall.middle(1)
    swap.begin()
    tall.begin(3)
    tall.end(0)
    for load in loads:
        load.wait()
    project(0)
    tall.end(1)
    tall.middle(2)
    swap.middle()
    project(1)
    queries.hop(0, 1)
    pairs.hop(0, 1)
    tall.middle(3)
    queries.hop(1, 1)
    pairs.hop(1, 1)
    tall.end(2)
    pairs.hop(0, 2)
    swap.end()
    shares.begin(0)
    project(2)
    tall.end(3)
    pairs.hop(0, 3)
    pairs.hop(1, 2)
    project(3)
    pairs.hop(2, 1)
    pairs.hop(1, 3)
    pairs.hop(3, 1)
    pairs.hop(2, 2)
    shares.hop(0, 1)
    pairs.hop(3, 2)
    queries.hop(2, 1)
    pairs.hop(2, 3)
    queries.hop(3, 1)
    pairs.hop(3, 3)
    for part in range(PARTS):
        queries.end(part)
        pairs.end(part)
    shares.end(0)
    tall.drain()
    swap.drain()
    queries.drain()
    pairs.drain()
    shares.drain()


def project(rows, count, w_query, w_key, w_value, w_out):
    width = rows.shape[1]
    deep = w_query.shape[0]
    share = w_out.shape[0] // NX
    dma = pltpu.SemaphoreType.DMA
    return pl.pallas_call(
        project_kernel,
        out_shape=(
            jax.ShapeDtypeStruct((NX, EXT, 256), BF16),
            jax.ShapeDtypeStruct((NZ, EXT, 256), BF16),
            jax.ShapeDtypeStruct((SLOTS, 128), F32),
            jax.ShapeDtypeStruct((NX, TP, share, width), BF16),
        ),
        in_specs=[VMEM, VMEM, FAR, FAR, FAR, FAR],
        out_specs=(VMEM, VMEM, VMEM, FAR),
        scratch_shapes=[
            pltpu.VMEM((TP, EXT, width), BF16),
            pltpu.VMEM((deep, 512), BF16),
            pltpu.VMEM((LARGEST, 512), F32),
            pltpu.VMEM((LARGEST, 128), F32),
            pltpu.VMEM((LARGEST, 128), F32),
            pltpu.VMEM((2, 2, share // 2, width), BF16),
            dma((PARTS * 9,)), dma((PARTS * 9,)),
            dma((PARTS * NZ,)), dma((PARTS * NZ,)),
            dma((PARTS * NX,)), dma((PARTS * NX,)),
            dma((13,)), dma((13,)),
            dma((NX,)), dma((NX,)),
            dma((5,)),
        ],
        compiler_params=pltpu.CompilerParams(
            collective_id=0, has_side_effects=True, vmem_limit_bytes=24 * MIB
        ),
        cost_estimate=pl.CostEstimate(flops=2 << 30, bytes_accessed=16 << 20, transcendentals=0),
        name="project",
    )(rows, count, w_query, w_key, w_value, w_out)


KEYS = 1024
QROWS = 512


def attend_kernel(
    query, pair, out, stats, kp, vp, qp, op, sp, top, accum, first_scores, second_scores, table, numbers, sem
):
    ctx = lax.axis_index("ctx")
    z, x = ctx // NX, ctx % NX

    heads = [query[at, :HEAD, :] for at in range(NX)] + [pair[at, :HEAD, :] for at in range(NZ)]
    for at, head in enumerate(heads):
        head = head.astype(F32)[0:1]
        table[at : at + 1, :] = (head[:, :128] * 16.0 + head[:, 128:]).astype(jnp.int32)
    read = pltpu.make_async_copy(table, numbers, sem)
    read.start()

    def padded(n):
        return (n + 15) // 16 * 16

    slot = lax.broadcasted_iota(jnp.int32, (SLOTS, 128), 0)
    lane = lax.broadcasted_iota(jnp.int32, (SLOTS, 128), 1)
    op[...] = jnp.zeros_like(op)
    sp[...] = jnp.zeros_like(sp)
    read.wait()

    q_from = []
    used = jnp.int32(0)
    for at in range(NX):
        rows = pl.ds(pl.multiple_of(used, 16), SLOTS)
        for head in range(2):
            scaled = query[at, HEAD:, head * 128 : (head + 1) * 128].astype(F32) * SCALE
            high = scaled.astype(BF16)
            qp[head, rows, :128] = high
            qp[head, rows, 128:] = (scaled - high.astype(F32)).astype(BF16)
        q_from.append(used)
        used = used + padded(numbers[at, 0])
    q_blocks = (used + QROWS - 1) // QROWS

    def pack(at, place, n):
        rows = pl.ds(pl.multiple_of(place, 16), SLOTS)
        valid = slot < n
        keys = pair[at, HEAD:, :128]
        first = jnp.broadcast_to(keys[0:1].astype(F32), (SLOTS, 128)).astype(BF16)
        keys = jnp.where(valid, keys, first)
        kp[rows, :128] = keys
        kp[rows, 128:] = keys
        vp[rows, :128] = pair[at, HEAD:, 128:]
        vp[rows, 128:] = jnp.where(valid & (lane == 0), 1.0, 0.0).astype(BF16)

    here = numbers[NX + z, 0]
    pack(z, jnp.int32(0), here)

    def earlier(at, place):
        n = numbers[NX + at, 0]
        pack(at, place, n)
        return place + padded(n)

    last = lax.fori_loop(0, z, earlier, jnp.int32(SLOTS))
    first = jnp.broadcast_to(kp[SLOTS : SLOTS + 16, :][0:1].astype(F32), (KEYS, 256)).astype(BF16)
    rows = pl.ds(pl.multiple_of(last, 16), KEYS)
    kp[rows, :] = first
    vp[rows, :] = jnp.zeros((KEYS, 256), BF16)
    k_blocks = (last - SLOTS + KEYS - 1) // KEYS

    mine = jnp.int32(0)
    for at in range(NX):
        mine = jnp.where(x == at, q_from[at], mine)

    def score(head, q_rows, k_rows):
        return lax.dot_general(
            qp[head, q_rows, :], kp[k_rows, :], (((1,), (1,)), ((), ())), preferred_element_type=F32
        )

    def absorb(head, scores, k_rows, mask=None):
        spot = slice(head * QROWS, (head + 1) * QROWS)
        if mask is not None:
            scores = jnp.where(mask, scores, -1e30)
        old = top[spot, :]
        new = jnp.maximum(old, jnp.max(scores, axis=1, keepdims=True))
        shrink = jnp.exp(old - new)
        expo = jnp.exp(scores - new[:, :1])
        top[spot, :] = new
        made = jnp.dot(expo.astype(BF16), vp[k_rows, :], preferred_element_type=F32)
        accum[spot, :128] = accum[spot, :128] * shrink + made[:, :128]
        accum[spot, 128:] = accum[spot, 128:] * shrink + made[:, 128:]

    def k_at(step):
        return pl.ds(pl.multiple_of(SLOTS + step * KEYS, 512), KEYS)

    def q_block(at, carry):
        begin = at * QROWS
        q_rows = pl.ds(pl.multiple_of(begin, QROWS), QROWS)
        top[...] = jnp.full_like(top, -1e29)
        accum[...] = jnp.zeros_like(accum)

        @pl.when(begin + QROWS > mine)
        def _():
            row = begin + lax.broadcasted_iota(jnp.int32, (QROWS, SLOTS), 0)
            key = lax.broadcasted_iota(jnp.int32, (QROWS, SLOTS), 1)
            mask = key < jnp.clip(row - mine + 1, 0, here)
            own = pl.ds(0, SLOTS)
            for head in range(2):
                absorb(head, score(head, q_rows, own), own, mask)

        @pl.when(k_blocks > 0)
        def _():
            first_scores[...] = score(0, q_rows, k_at(0))

        def k_block(step, carry):
            second_scores[...] = score(1, q_rows, k_at(step))
            absorb(0, first_scores[...], k_at(step))
            first_scores[...] = score(0, q_rows, k_at(jnp.minimum(step + 1, k_blocks - 1)))
            absorb(1, second_scores[...], k_at(step))
            return carry

        lax.fori_loop(0, k_blocks, k_block, 0)
        spot = lax.broadcasted_iota(jnp.int32, (QROWS, 128), 1)
        kept = jnp.zeros((QROWS, 128), F32)
        for head in range(2):
            part = slice(head * QROWS, (head + 1) * QROWS)
            whole = accum[part, 128:129]
            op[q_rows, head * 128 : (head + 1) * 128] = (
                accum[part, :128] / jnp.maximum(whole, 1e-30)
            ).astype(BF16)
            kept = jnp.where(spot == 2 * head, top[part, :], kept)
            kept = jnp.where(spot == 2 * head + 1, whole, kept)
        sp[q_rows, :] = kept
        return carry

    lax.fori_loop(0, q_blocks, q_block, 0)
    for at in range(NX):
        rows = pl.ds(pl.multiple_of(q_from[at], 16), SLOTS)
        out[at] = op[rows, :]
        stats[at] = jnp.transpose(sp[rows, :])[:8]


def attend(query, pair):
    packed_q = (NX + 1) * SLOTS
    packed_k = (NZ + 1) * SLOTS + KEYS
    return pl.pallas_call(
        attend_kernel,
        out_shape=(
            jax.ShapeDtypeStruct((NX, SLOTS, 256), BF16),
            jax.ShapeDtypeStruct((NX, 8, SLOTS), F32),
        ),
        in_specs=[VMEM, VMEM],
        out_specs=(VMEM, VMEM),
        scratch_shapes=[
            pltpu.VMEM((packed_k, 256), BF16),
            pltpu.VMEM((packed_k, 256), BF16),
            pltpu.VMEM((2, packed_q, 256), BF16),
            pltpu.VMEM((packed_q, 256), BF16),
            pltpu.VMEM((packed_q, 128), F32),
            pltpu.VMEM((2 * QROWS, 128), F32),
            pltpu.VMEM((2 * QROWS, 256), F32),
            pltpu.VMEM((QROWS, KEYS), F32),
            pltpu.VMEM((QROWS, KEYS), F32),
            pltpu.VMEM((16, 128), jnp.int32),
            pltpu.SMEM((16, 128), jnp.int32),
            pltpu.SemaphoreType.DMA,
        ],
        compiler_params=pltpu.CompilerParams(vmem_limit_bytes=28 * MIB),
        cost_estimate=pl.CostEstimate(flops=4 << 30, bytes_accessed=8 << 20, transcendentals=4 << 20),
        name="attend",
    )(query, pair)


def merge_kernel(
    part_out, stats, gate, columns, update,
    came, came_stats, relay, own, held, weights, total,
    x_send, x_recv, s_send, s_recv, a_send, a_recv, local_sem,
):
    ctx, tp = lax.axis_index("ctx"), lax.axis_index("tp")
    z, x = ctx // NX, ctx % NX
    right, left, far = (x + 1) % NX, (x + NX - 1) % NX, (x + 2) % NX

    def at_x(at):
        return (z * NX + at, tp)

    spans = [(part * ROWS, ROWS) for part in range(MERGES)]
    gather = TpGather(own, held, (a_send, a_recv), spans)
    share = columns.shape[2]
    loads = [
        pltpu.make_async_copy(columns.at[at], weights.at[:, pl.ds(at * share, share)], local_sem.at[at])
        for at in range(NX)
    ]
    for load in loads:
        load.start()
    greet(gather.partners + [at_x(right), at_x(left), at_x(far)])

    copies = {}

    def send(part, item, src, dst, device):
        copy = remote(src, dst, (x_send, x_recv), part * 6 + item, device)
        copy.start()
        copies[part, item] = copy

    told = []
    for item, to in enumerate((right, left, far)):
        copy = remote(stats.at[to], came_stats.at[x], (s_send, s_recv), item, at_x(to))
        copy.start()
        told.append(copy)

    def begin(part):
        rows = spans[part]
        low, high = halves(*rows)
        send(part, 2, part_out.at[far, pl.ds(*low)], relay.at[part, 0], at_x(right))
        send(part, 3, part_out.at[far, pl.ds(*high)], relay.at[part, 1], at_x(left))
        send(part, 0, part_out.at[right, pl.ds(*rows)], came.at[x, pl.ds(*rows)], at_x(right))
        send(part, 1, part_out.at[left, pl.ds(*rows)], came.at[x, pl.ds(*rows)], at_x(left))

    def middle(part):
        low, high = halves(*spans[part])
        copies[part, 2].wait_recv()
        send(part, 4, relay.at[part, 0], came.at[left, pl.ds(*low)], at_x(right))
        copies[part, 3].wait_recv()
        send(part, 5, relay.at[part, 1], came.at[right, pl.ds(*high)], at_x(left))

    def combine(part):
        for item in (0, 1, 4, 5):
            copies[part, item].wait_recv()
        lo = part * ROWS
        lines = [stats[x, :, lo : lo + ROWS]] + [
            came_stats[at, :, lo : lo + ROWS] for at in (right, left, far)
        ]
        shares = []
        for head in range(2):
            tops = [line[2 * head : 2 * head + 1] for line in lines]
            best = functools.reduce(jnp.maximum, tops)
            mass = [
                line[2 * head + 1 : 2 * head + 2] * jnp.exp(one - best)
                for line, one in zip(lines, tops)
            ]
            whole = jnp.maximum(sum(mass), 1e-30)
            shares += [one / whole for one in mass]
        turned = jnp.transpose(
            jnp.concatenate(shares + [jnp.zeros((120, ROWS), F32)], axis=0)
        )
        blocks = [part_out[x, lo : lo + ROWS, :]] + [
            came[at, lo : lo + ROWS, :] for at in (right, left, far)
        ]
        for head in range(2):
            mixed = sum(
                block[:, head * 128 : (head + 1) * 128].astype(F32)
                * turned[:, head * 4 + i : head * 4 + i + 1]
                for i, block in enumerate(blocks)
            ).astype(BF16)
            own[lo : lo + ROWS, head * 128 : (head + 1) * 128] = mixed
            held[tp, lo : lo + ROWS, head * 128 : (head + 1) * 128] = mixed

    def finish(lo):
        total[...] = jnp.zeros_like(total)

        @pl.loop(0, TP)
        def _(slot):
            total[...] += jnp.dot(
                held[slot, lo : lo + DONE, :], weights[slot], preferred_element_type=F32
            )

        update[lo : lo + DONE, :] = (total[...] * gate[lo : lo + DONE, :1]).astype(BF16)

    def pass_on(part):
        combine(part)
        gather.begin(part)

    begin(0)
    middle(0)
    begin(1)
    for copy in told:
        copy.wait_recv()
    pass_on(0)
    middle(1)
    gather.middle(0)
    pass_on(1)
    gather.end(0)
    for load in loads:
        load.wait()
    gather.middle(1)
    finish(0)
    gather.end(1)
    finish(DONE)
    for copy in told + list(copies.values()):
        copy.wait_send()
    gather.drain()


def merge(part_out, stats, gate, columns):
    share, width = columns.shape[2:]
    dma = pltpu.SemaphoreType.DMA
    return pl.pallas_call(
        merge_kernel,
        out_shape=jax.ShapeDtypeStruct((SLOTS, width), BF16),
        in_specs=[VMEM, VMEM, VMEM, FAR],
        out_specs=VMEM,
        scratch_shapes=[
            pltpu.VMEM((NX, SLOTS, 256), BF16),
            pltpu.VMEM((NX, 8, SLOTS), F32),
            pltpu.VMEM((MERGES, 2, ROWS // 2, 256), BF16),
            pltpu.VMEM((SLOTS, 256), BF16),
            pltpu.VMEM((TP, SLOTS, 256), BF16),
            pltpu.VMEM((TP, NX * share, width), BF16),
            pltpu.VMEM((DONE, width), F32),
            dma((MERGES * 6,)), dma((MERGES * 6,)),
            dma((3,)), dma((3,)),
            dma((MERGES * 9,)), dma((MERGES * 9,)),
            dma((NX,)),
        ],
        compiler_params=pltpu.CompilerParams(
            collective_id=1, has_side_effects=True, vmem_limit_bytes=20 * MIB
        ),
        cost_estimate=pl.CostEstimate(flops=1 << 30, bytes_accessed=8 << 20, transcendentals=0),
        name="merge",
    )(part_out, stats, gate, columns)


def spread_kernel(tokens, rank, update, out):
    turned = jnp.transpose(rank[...])
    slot = lax.broadcasted_iota(jnp.int32, (128, SLOTS), 1).astype(F32)
    for b in range(rank.shape[0]):
        place = jnp.where(turned[:, b : b + 1] == slot, 1.0, 0.0).astype(BF16)
        added = jnp.dot(place, update[...], preferred_element_type=F32)
        rows = slice(b * 128, (b + 1) * 128)
        out[rows, :] = (tokens[rows, :].astype(F32) + added).astype(BF16)


def spread(tokens, rank, update):
    tall, width = tokens.shape
    steps = rank.shape[0] // 8
    return pl.pallas_call(
        spread_kernel,
        out_shape=jax.ShapeDtypeStruct((tall, width), BF16),
        grid=(steps,),
        in_specs=[
            pl.BlockSpec((tall // steps, width), lambda i: (i, 0)),
            pl.BlockSpec((8, 128), lambda i: (i, 0)),
            pl.BlockSpec((SLOTS, width), lambda i: (0, 0)),
        ],
        out_specs=pl.BlockSpec((tall // steps, width), lambda i: (i, 0)),
        compiler_params=pltpu.CompilerParams(vmem_limit_bytes=12 * MIB),
        cost_estimate=pl.CostEstimate(flops=1 << 30, bytes_accessed=5 << 20, transcendentals=0),
        name="spread",
    )(tokens, rank, update)


def body(tokens, block_counts, block_orders, w_router, w_query, w_key, w_value, w_out):
    far = [
        pltpu.with_memory_space_constraint(array, pltpu.HBM)
        for array in (tokens, block_counts, block_orders, w_router, w_query, w_key, w_value, w_out)
    ]
    rows, rank, count = route(*far[:4])
    query, pair, gate, columns = project(rows, count, *far[4:])
    part_out, stats = attend(query, pair)
    update = merge(part_out, stats, gate, columns)
    return spread(tokens, rank, update)


def solution(mesh):
    return jax.shard_map(
        body,
        mesh=mesh,
        in_specs=(
            P("ctx", "tp"),
            P("ctx"),
            P("ctx", None),
            P("tp"),
            P(None, "tp"),
            P(None, "tp"),
            P(None, "tp"),
            P("tp", None),
        ),
        out_specs=P("ctx", "tp"),
        check_vma=False,
    )
```

```python
import functools

import jax
import jax.numpy as jnp
from jax import lax
from jax.experimental import pallas as pl
from jax.experimental.pallas import tpu as pltpu
from jax.sharding import PartitionSpec as P

NX, NY, NZ = 4, 4, 8
TP = 2 * NY
SLOTS = 512
PICK = 32
HEAD = 16
EXT = HEAD + SLOTS
HD = 128
SLOT_SPANS = [(0, 128), (128, 128), (256, 128), (384, 128)]
SPANS = [(0, HEAD + 128)] + [(HEAD + at, size) for at, size in SLOT_SPANS[1:]]
PARTS = len(SPANS)
LARGEST = 128
MERGES = 2
ROWS = SLOTS // MERGES
DONE = 256
SCALE = HD ** (-0.5)
MESH = pl.DeviceIdType.MESH
F32, BF16 = jnp.float32, jnp.bfloat16
VMEM = pl.BlockSpec(memory_space=pltpu.VMEM)
FAR = pl.BlockSpec(memory_space=pltpu.HBM)
MIB = 1 << 20


def halves(start, size, unit=16):
    first = -(-(size // 2) // unit) * unit
    return (start, first), (start + first, size - first)


def remote(src, dst, sems, item, device):
    return pltpu.make_async_remote_copy(
        src_ref=src, dst_ref=dst, send_sem=sems[0].at[item], recv_sem=sems[1].at[item],
        device_id=device, device_id_type=MESH,
    )


def greet(partners):
    barrier = pltpu.get_barrier_semaphore()
    for device in partners:
        pl.semaphore_signal(barrier, inc=1, device_id=device, device_id_type=MESH)


def await_greetings(partners):
    pl.semaphore_wait(pltpu.get_barrier_semaphore(), len(partners))


def pick_rows(counts, tokens, orders, arrivals, rows, rank, pick, total):
    blocks = orders.shape[0]
    turned = jnp.transpose(orders[...].astype(F32))
    lane = lax.broadcasted_iota(jnp.int32, (PICK, 128), 1).astype(F32)
    slot = lax.broadcasted_iota(jnp.int32, (PICK, 128), 0)
    chosen = []
    for b in range(blocks):
        hit = (turned[:PICK, b : b + 1] == lane) & (slot < counts[b])
        chosen.append(jnp.sum(jnp.where(hit, 1.0, 0.0), axis=0, keepdims=True))
    upper = (
        lax.broadcasted_iota(jnp.int32, (128, 128), 0) < lax.broadcasted_iota(jnp.int32, (128, 128), 1)
    )
    chosen = jnp.concatenate(chosen, axis=0)
    within = jnp.dot(
        chosen.astype(BF16), jnp.where(upper, 1.0, 0.0).astype(BF16), preferred_element_type=F32
    )
    before = jnp.int32(0)
    index = lax.broadcasted_iota(jnp.int32, (SLOTS, 128), 0).astype(F32)
    for b in range(blocks):
        line = jnp.where(
            chosen[b : b + 1] > 0.5, within[b : b + 1] + before.astype(F32), -1.0
        )
        rank[b : b + 1, :] = line
        pick[:, b * 128 : (b + 1) * 128] = jnp.where(index == line, 1.0, 0.0).astype(BF16)
        before = before + counts[b]
    tall = tokens.shape[0] // len(arrivals)
    for at, copy in enumerate(arrivals):
        copy.wait()
        some = slice(at * tall, (at + 1) * tall)
        made = jnp.dot(pick[:, some], tokens[some, :], preferred_element_type=F32)
        if at == 0:
            total[...] = made
        elif at < len(arrivals) - 1:
            total[...] += made
        else:
            rows[...] = (total[...] + made).astype(BF16)
    return before


class TpGather:
    def __init__(self, own, held, sems, spans):
        tp, ctx = lax.axis_index("tp"), lax.axis_index("ctx")
        y, core = tp // 2, tp % 2
        self.own, self.held, self.sems, self.spans, self.tp = own, held, sems, spans, tp
        self.up_slot = ((y + 1) % NY) * 2 + core
        self.down_slot = ((y + NY - 1) % NY) * 2 + core
        self.far_slot = ((y + 2) % NY) * 2 + core
        self.up, self.down = (ctx, self.up_slot), (ctx, self.down_slot)
        self.sibling = (ctx, y * 2 + 1 - core)
        self.partners = [self.up, self.down, self.sibling]
        self.copies = {}

    def send(self, part, item, src, slot, rows, device):
        copy = remote(
            src.at[pl.ds(*rows)], self.held.at[slot, pl.ds(*rows)], self.sems, part * 9 + item, device
        )
        copy.start()
        self.copies[part, item] = copy

    def begin(self, part):
        rows = self.spans[part]
        self.send(part, 0, self.own, self.tp, rows, self.up)
        self.send(part, 1, self.own, self.tp, rows, self.down)
        self.send(part, 2, self.own, self.tp, rows, self.sibling)

    def middle(self, part):
        rows = self.spans[part]
        low, high = halves(*rows)
        self.copies[part, 0].wait_recv()
        self.send(part, 3, self.held.at[self.down_slot], self.down_slot, low, self.up)
        self.send(part, 5, self.held.at[self.down_slot], self.down_slot, rows, self.sibling)
        self.copies[part, 1].wait_recv()
        self.send(part, 4, self.held.at[self.up_slot], self.up_slot, high, self.down)
        self.send(part, 6, self.held.at[self.up_slot], self.up_slot, rows, self.sibling)

    def end(self, part):
        low, high = halves(*self.spans[part])
        self.copies[part, 3].wait_recv()
        self.send(part, 7, self.held.at[self.far_slot], self.far_slot, low, self.sibling)
        self.copies[part, 4].wait_recv()
        self.send(part, 8, self.held.at[self.far_slot], self.far_slot, high, self.sibling)

    def settle(self, part):
        for item in (2, 5, 6, 7, 8):
            self.copies[part, item].wait_recv()

    def drain(self):
        for copy in self.copies.values():
            copy.wait_send()


class RingGather:
    def __init__(self, held, sems, spans, me, size, device_of, unit=16):
        self.held, self.sems, self.spans, self.me, self.size = held, sems, spans, me, size
        self.up, self.down = device_of((me + 1) % size), device_of((me + size - 1) % size)
        self.partners = [self.up, self.down]
        self.unit = unit
        self.copies = {}

    def send(self, part, hop, way, slot, rows):
        item = hop * 2 + way
        at = self.held.at[slot, pl.ds(*rows)]
        copy = remote(at, at, self.sems, part * self.size + item, self.down if way else self.up)
        copy.start()
        self.copies[part, item] = copy

    def begin(self, part):
        self.send(part, 0, 0, self.me, self.spans[part])
        self.send(part, 0, 1, self.me, self.spans[part])

    def hop(self, part, hop):
        rows = self.spans[part]
        low, high = halves(*rows, self.unit)
        last = hop == self.size // 2 - 1
        self.copies[part, hop * 2 - 2].wait_recv()
        self.send(part, hop, 0, (self.me + self.size - hop) % self.size, low if last else rows)
        self.copies[part, hop * 2 - 1].wait_recv()
        self.send(part, hop, 1, (self.me + hop) % self.size, high if last else rows)

    def end(self, part):
        self.copies[part, self.size - 2].wait_recv()
        self.copies[part, self.size - 1].wait_recv()

    def drain(self):
        for copy in self.copies.values():
            copy.wait_send()


class Swap:
    def __init__(self, matrix, held, relay, sems, first):
        tp, ctx = lax.axis_index("tp"), lax.axis_index("ctx")
        self.y, self.core, self.tp, self.ctx = tp // 2, tp % 2, tp, ctx
        self.matrix, self.held, self.relay, self.sems = matrix, held, relay, sems
        self.depth, self.width = held.shape[1], held.shape[2]
        self.first = first
        self.copies = {}
        self.cores = [self.core, 1 - self.core]
        self.partners = [self.device(step, core) for step in (1, NY - 1) for core in self.cores]
        self.partners.append((ctx, self.y * 2 + 1 - self.core))

    def slot(self, step, core):
        return ((self.y + step) % NY) * 2 + core

    def device(self, step, core):
        return (self.ctx, self.slot(step, core))

    def block(self, slot, rows):
        start, size = rows
        rows = pl.ds(pl.multiple_of(self.first + start, 16), size)
        return self.matrix.at[rows, pl.ds(pl.multiple_of(slot * self.width, 512), self.width)]

    def send(self, item, src, dst, device):
        copy = remote(src, dst, self.sems, item, device)
        copy.start()
        self.copies[item] = copy

    def begin(self):
        whole, half = (0, self.depth), self.depth // 2
        sibling = self.y * 2 + 1 - self.core
        for way, step in enumerate((1, NY - 1)):
            for i, core in enumerate(self.cores):
                far = self.slot(2, core)
                self.send(
                    way * 2 + i, self.block(far, (way * half, half)), self.relay.at[way, i],
                    self.device(step, self.core),
                )
        for way, step in enumerate((1, NY - 1)):
            for i, core in enumerate(self.cores):
                self.send(
                    4 + way * 2 + i, self.block(self.slot(step, core), whole), self.held.at[self.tp],
                    self.device(step, core),
                )
        self.send(12, self.block(sibling, whole), self.held.at[self.tp], (self.ctx, sibling))

    def middle(self):
        half = self.depth // 2
        for way, step in enumerate((1, NY - 1)):
            source = self.slot(NY - step, self.core)
            for i, core in enumerate(self.cores):
                self.copies[way * 2 + i].wait_recv()
                self.send(
                    8 + way * 2 + i, self.relay.at[way, i],
                    self.held.at[source, pl.ds(way * half, half)], self.device(step, core),
                )

    def end(self):
        for item in range(4, 13):
            self.copies[item].wait_recv()

    def drain(self):
        for copy in self.copies.values():
            copy.wait_send()


def project_kernel(
    far_tokens, far_counts, far_orders, router, w_query, w_key, w_value, w_out,
    query, pair, gate, columns, rank,
    counts, tokens, orders, pick, gathered, held, weights, total, square, score, relay,
    a_send, a_recv, z_send, z_recv, x_send, x_recv, w_send, w_recv, c_send, c_recv, local_sem,
):
    ctx, tp = lax.axis_index("ctx"), lax.axis_index("tp")
    z, x = ctx // NX, ctx % NX
    depth, width = columns.shape[2:]
    inner = weights.shape[0] // TP
    tall = TpGather(held.at[tp], held, (a_send, a_recv), SPANS)
    pairs = RingGather(pair, (z_send, z_recv), SPANS, z, NZ, lambda at: (at * NX + x, tp))
    queries = RingGather(query, (x_send, x_recv), SPANS, x, NX, lambda at: (z * NX + at, tp))
    swap = Swap(w_out, columns.at[x], relay, (w_send, w_recv), x * depth)
    shares = RingGather(
        columns, (c_send, c_recv), [(0, TP)], x, NX, lambda at: (z * NX + at, tp), 1
    )

    partners = pairs.partners + queries.partners + swap.partners
    greet(partners)
    small = [
        pltpu.make_async_copy(far_counts, counts, local_sem.at[4]),
        pltpu.make_async_copy(far_orders, orders, local_sem.at[5]),
    ]
    quarter = tokens.shape[0] // 4
    large = [
        pltpu.make_async_copy(
            far_tokens.at[pl.ds(at * quarter, quarter)],
            tokens.at[pl.ds(at * quarter, quarter)],
            local_sem.at[6 + at],
        )
        for at in range(4)
    ]
    loads = [
        pltpu.make_async_copy(w_query, weights.at[:, pl.ds(0, 256)], local_sem.at[0]),
        pltpu.make_async_copy(w_key, weights.at[:, pl.ds(256, 128)], local_sem.at[1]),
        pltpu.make_async_copy(w_value, weights.at[:, pl.ds(384, 128)], local_sem.at[2]),
        pltpu.make_async_copy(
            w_out.at[
                pl.ds(pl.multiple_of(x * depth, 16), depth),
                pl.ds(pl.multiple_of(tp * width, 512), width),
            ],
            columns.at[x, tp],
            local_sem.at[3],
        ),
    ]
    for load in small + large + loads:
        load.start()
    for load in small:
        load.wait()
    held[tp, :HEAD, :] = jnp.broadcast_to(router[...].reshape(1, width), (HEAD, width))
    number = pick_rows(
        counts, tokens, orders, large, held.at[tp, pl.ds(HEAD, SLOTS)], rank, pick, gathered
    )
    high = number // 16
    for ref in (query.at[x], pair.at[z]):
        ref[:HEAD, :128] = jnp.full((HEAD, 128), high.astype(F32), F32).astype(BF16)
        ref[:HEAD, 128:] = jnp.full((HEAD, 128), (number - high * 16).astype(F32), F32).astype(BF16)
    await_greetings(partners)

    def project(part):
        start, size = SLOT_SPANS[part]
        start += HEAD
        here = slice(0, size)
        tall.settle(part)
        total[here, :] = jnp.zeros((size, 512), F32)
        square[here, :] = jnp.zeros((size, 128), F32)
        score[here, :] = jnp.zeros((size, 128), F32)

        @pl.loop(0, TP)
        def _(slot):
            block = held[slot, start : start + size, :]
            deep = pl.ds(pl.multiple_of(slot * inner, 512), inner)
            total[here, :] += jnp.dot(block, weights[deep, :], preferred_element_type=F32)
            router = held[slot, 0:HEAD, :].astype(F32)[0:1]
            wide = block.astype(F32)
            both, dots = wide * wide, wide * router
            square[here, :] += sum(both[:, c : c + 128] for c in range(0, inner, 128))
            score[here, :] += sum(dots[:, c : c + 128] for c in range(0, inner, 128))

        inv = lax.rsqrt(jnp.sum(square[here, :], axis=1, keepdims=True) / weights.shape[0] + 1e-05)
        open_ = jax.nn.sigmoid(jnp.sum(score[here, :], axis=1, keepdims=True))
        gate[start - HEAD : start - HEAD + size, :] = jnp.broadcast_to(open_, (size, 128))
        query[x, start : start + size, :] = (total[here, :256] * inv).astype(BF16)
        pair[z, start : start + size, :] = (total[here, 256:] * inv).astype(BF16)
        pairs.begin(part)
        queries.begin(part)

    tall.begin(0)
    tall.begin(1)
    tall.middle(0)
    tall.begin(2)
    tall.middle(1)
    swap.begin()
    tall.begin(3)
    tall.end(0)
    for load in loads:
        load.wait()
    project(0)
    tall.end(1)
    tall.middle(2)
    swap.middle()
    project(1)
    queries.hop(0, 1)
    pairs.hop(0, 1)
    tall.middle(3)
    queries.hop(1, 1)
    pairs.hop(1, 1)
    tall.end(2)
    pairs.hop(0, 2)
    swap.end()
    shares.begin(0)
    project(2)
    tall.end(3)
    pairs.hop(0, 3)
    pairs.hop(1, 2)
    project(3)
    pairs.hop(2, 1)
    pairs.hop(1, 3)
    pairs.hop(3, 1)
    pairs.hop(2, 2)
    shares.hop(0, 1)
    pairs.hop(3, 2)
    queries.hop(2, 1)
    pairs.hop(2, 3)
    queries.hop(3, 1)
    pairs.hop(3, 3)
    for part in range(PARTS):
        queries.end(part)
        pairs.end(part)
    shares.end(0)
    tall.drain()
    swap.drain()
    queries.drain()
    pairs.drain()
    shares.drain()


def project(tokens, counts, orders, router, w_query, w_key, w_value, w_out):
    tall, width = tokens.shape
    deep = w_query.shape[0]
    share = w_out.shape[0] // NX
    dma = pltpu.SemaphoreType.DMA
    return pl.pallas_call(
        project_kernel,
        out_shape=(
            jax.ShapeDtypeStruct((NX, EXT, 256), BF16),
            jax.ShapeDtypeStruct((NZ, EXT, 256), BF16),
            jax.ShapeDtypeStruct((SLOTS, 128), F32),
            jax.ShapeDtypeStruct((NX, TP, share, width), BF16),
            jax.ShapeDtypeStruct(orders.shape, F32),
        ),
        in_specs=[FAR, FAR, FAR, VMEM, FAR, FAR, FAR, FAR],
        out_specs=(VMEM, VMEM, VMEM, FAR, VMEM),
        scratch_shapes=[
            pltpu.SMEM(counts.shape, jnp.int32),
            pltpu.VMEM(tokens.shape, BF16),
            pltpu.VMEM(orders.shape, jnp.int32),
            pltpu.VMEM((SLOTS, tall), BF16),
            pltpu.VMEM((SLOTS, width), F32),
            pltpu.VMEM((TP, EXT, width), BF16),
            pltpu.VMEM((deep, 512), BF16),
            pltpu.VMEM((LARGEST, 512), F32),
            pltpu.VMEM((LARGEST, 128), F32),
            pltpu.VMEM((LARGEST, 128), F32),
            pltpu.VMEM((2, 2, share // 2, width), BF16),
            dma((PARTS * 9,)), dma((PARTS * 9,)),
            dma((PARTS * NZ,)), dma((PARTS * NZ,)),
            dma((PARTS * NX,)), dma((PARTS * NX,)),
            dma((13,)), dma((13,)),
            dma((NX,)), dma((NX,)),
            dma((10,)),
        ],
        compiler_params=pltpu.CompilerParams(
            collective_id=0, has_side_effects=True, vmem_limit_bytes=28 * MIB
        ),
        cost_estimate=pl.CostEstimate(flops=2 << 30, bytes_accessed=16 << 20, transcendentals=0),
        name="project",
    )(tokens, counts, orders, router, w_query, w_key, w_value, w_out)


KEYS = 1024
QROWS = 512


def attend_kernel(
    query, pair, out, stats, kp, vp, qp, op, sp, top, accum, first_scores, second_scores, table, numbers, sem
):
    ctx = lax.axis_index("ctx")
    z, x = ctx // NX, ctx % NX

    heads = [query[at, :HEAD, :] for at in range(NX)] + [pair[at, :HEAD, :] for at in range(NZ)]
    for at, head in enumerate(heads):
        head = head.astype(F32)[0:1]
        table[at : at + 1, :] = (head[:, :128] * 16.0 + head[:, 128:]).astype(jnp.int32)
    read = pltpu.make_async_copy(table, numbers, sem)
    read.start()

    def padded(n):
        return (n + 15) // 16 * 16

    slot = lax.broadcasted_iota(jnp.int32, (SLOTS, 128), 0)
    lane = lax.broadcasted_iota(jnp.int32, (SLOTS, 128), 1)
    op[...] = jnp.zeros_like(op)
    sp[...] = jnp.zeros_like(sp)
    read.wait()

    q_from = []
    used = jnp.int32(0)
    for at in range(NX):
        rows = pl.ds(pl.multiple_of(used, 16), SLOTS)
        for head in range(2):
            scaled = query[at, HEAD:, head * 128 : (head + 1) * 128].astype(F32) * SCALE
            high = scaled.astype(BF16)
            qp[head, rows, :128] = high
            qp[head, rows, 128:] = (scaled - high.astype(F32)).astype(BF16)
        q_from.append(used)
        used = used + padded(numbers[at, 0])
    q_blocks = (used + QROWS - 1) // QROWS

    def pack(at, place, n):
        rows = pl.ds(pl.multiple_of(place, 16), SLOTS)
        valid = slot < n
        keys = pair[at, HEAD:, :128]
        first = jnp.broadcast_to(keys[0:1].astype(F32), (SLOTS, 128)).astype(BF16)
        keys = jnp.where(valid, keys, first)
        kp[rows, :128] = keys
        kp[rows, 128:] = keys
        vp[rows, :128] = pair[at, HEAD:, 128:]
        vp[rows, 128:] = jnp.where(valid & (lane == 0), 1.0, 0.0).astype(BF16)

    here = numbers[NX + z, 0]
    pack(z, jnp.int32(0), here)

    def earlier(at, place):
        n = numbers[NX + at, 0]
        pack(at, place, n)
        return place + padded(n)

    last = lax.fori_loop(0, z, earlier, jnp.int32(SLOTS))
    first = jnp.broadcast_to(kp[SLOTS : SLOTS + 16, :][0:1].astype(F32), (KEYS, 256)).astype(BF16)
    rows = pl.ds(pl.multiple_of(last, 16), KEYS)
    kp[rows, :] = first
    vp[rows, :] = jnp.zeros((KEYS, 256), BF16)
    k_blocks = (last - SLOTS + KEYS - 1) // KEYS

    mine = jnp.int32(0)
    for at in range(NX):
        mine = jnp.where(x == at, q_from[at], mine)

    def score(head, q_rows, k_rows):
        return lax.dot_general(
            qp[head, q_rows, :], kp[k_rows, :], (((1,), (1,)), ((), ())), preferred_element_type=F32
        )

    def absorb(head, scores, k_rows, mask=None):
        spot = slice(head * QROWS, (head + 1) * QROWS)
        if mask is not None:
            scores = jnp.where(mask, scores, -1e30)
        old = top[spot, :]
        new = jnp.maximum(old, jnp.max(scores, axis=1, keepdims=True))
        shrink = jnp.exp(old - new)
        expo = jnp.exp(scores - new[:, :1])
        top[spot, :] = new
        made = jnp.dot(expo.astype(BF16), vp[k_rows, :], preferred_element_type=F32)
        accum[spot, :128] = accum[spot, :128] * shrink + made[:, :128]
        accum[spot, 128:] = accum[spot, 128:] * shrink + made[:, 128:]

    def k_at(step):
        return pl.ds(pl.multiple_of(SLOTS + step * KEYS, 512), KEYS)

    def q_block(at, carry):
        begin = at * QROWS
        q_rows = pl.ds(pl.multiple_of(begin, QROWS), QROWS)
        top[...] = jnp.full_like(top, -1e29)
        accum[...] = jnp.zeros_like(accum)

        @pl.when(begin + QROWS > mine)
        def _():
            row = begin + lax.broadcasted_iota(jnp.int32, (QROWS, SLOTS), 0)
            key = lax.broadcasted_iota(jnp.int32, (QROWS, SLOTS), 1)
            mask = key < jnp.clip(row - mine + 1, 0, here)
            own = pl.ds(0, SLOTS)
            for head in range(2):
                absorb(head, score(head, q_rows, own), own, mask)

        @pl.when(k_blocks > 0)
        def _():
            first_scores[...] = score(0, q_rows, k_at(0))

        def k_block(step, carry):
            second_scores[...] = score(1, q_rows, k_at(step))
            absorb(0, first_scores[...], k_at(step))
            first_scores[...] = score(0, q_rows, k_at(jnp.minimum(step + 1, k_blocks - 1)))
            absorb(1, second_scores[...], k_at(step))
            return carry

        lax.fori_loop(0, k_blocks, k_block, 0)
        spot = lax.broadcasted_iota(jnp.int32, (QROWS, 128), 1)
        kept = jnp.zeros((QROWS, 128), F32)
        for head in range(2):
            part = slice(head * QROWS, (head + 1) * QROWS)
            whole = accum[part, 128:129]
            op[q_rows, head * 128 : (head + 1) * 128] = (
                accum[part, :128] / jnp.maximum(whole, 1e-30)
            ).astype(BF16)
            kept = jnp.where(spot == 2 * head, top[part, :], kept)
            kept = jnp.where(spot == 2 * head + 1, whole, kept)
        sp[q_rows, :] = kept
        return carry

    lax.fori_loop(0, q_blocks, q_block, 0)
    for at in range(NX):
        rows = pl.ds(pl.multiple_of(q_from[at], 16), SLOTS)
        out[at] = op[rows, :]
        stats[at] = jnp.transpose(sp[rows, :])[:8]


def attend(query, pair):
    packed_q = (NX + 1) * SLOTS
    packed_k = (NZ + 1) * SLOTS + KEYS
    return pl.pallas_call(
        attend_kernel,
        out_shape=(
            jax.ShapeDtypeStruct((NX, SLOTS, 256), BF16),
            jax.ShapeDtypeStruct((NX, 8, SLOTS), F32),
        ),
        in_specs=[VMEM, VMEM],
        out_specs=(VMEM, VMEM),
        scratch_shapes=[
            pltpu.VMEM((packed_k, 256), BF16),
            pltpu.VMEM((packed_k, 256), BF16),
            pltpu.VMEM((2, packed_q, 256), BF16),
            pltpu.VMEM((packed_q, 256), BF16),
            pltpu.VMEM((packed_q, 128), F32),
            pltpu.VMEM((2 * QROWS, 128), F32),
            pltpu.VMEM((2 * QROWS, 256), F32),
            pltpu.VMEM((QROWS, KEYS), F32),
            pltpu.VMEM((QROWS, KEYS), F32),
            pltpu.VMEM((16, 128), jnp.int32),
            pltpu.SMEM((16, 128), jnp.int32),
            pltpu.SemaphoreType.DMA,
        ],
        compiler_params=pltpu.CompilerParams(vmem_limit_bytes=28 * MIB),
        cost_estimate=pl.CostEstimate(flops=4 << 30, bytes_accessed=8 << 20, transcendentals=4 << 20),
        name="attend",
    )(query, pair)


def merge_kernel(
    part_out, stats, gate, columns, update,
    came, came_stats, relay, own, held, weights, total,
    x_send, x_recv, s_send, s_recv, a_send, a_recv, local_sem,
):
    ctx, tp = lax.axis_index("ctx"), lax.axis_index("tp")
    z, x = ctx // NX, ctx % NX
    right, left, far = (x + 1) % NX, (x + NX - 1) % NX, (x + 2) % NX

    def at_x(at):
        return (z * NX + at, tp)

    spans = [(part * ROWS, ROWS) for part in range(MERGES)]
    gather = TpGather(own, held, (a_send, a_recv), spans)
    share = columns.shape[2]
    loads = [
        pltpu.make_async_copy(columns.at[at], weights.at[:, pl.ds(at * share, share)], local_sem.at[at])
        for at in range(NX)
    ]
    for load in loads:
        load.start()
    partners = gather.partners + [at_x(right), at_x(left), at_x(far)]
    greet(partners)
    await_greetings(partners)

    copies = {}

    def send(part, item, src, dst, device):
        copy = remote(src, dst, (x_send, x_recv), part * 6 + item, device)
        copy.start()
        copies[part, item] = copy

    told = []
    for item, to in enumerate((right, left, far)):
        copy = remote(stats.at[to], came_stats.at[x], (s_send, s_recv), item, at_x(to))
        copy.start()
        told.append(copy)

    def begin(part):
        rows = spans[part]
        low, high = halves(*rows)
        send(part, 2, part_out.at[far, pl.ds(*low)], relay.at[part, 0], at_x(right))
        send(part, 3, part_out.at[far, pl.ds(*high)], relay.at[part, 1], at_x(left))
        send(part, 0, part_out.at[right, pl.ds(*rows)], came.at[x, pl.ds(*rows)], at_x(right))
        send(part, 1, part_out.at[left, pl.ds(*rows)], came.at[x, pl.ds(*rows)], at_x(left))

    def middle(part):
        low, high = halves(*spans[part])
        copies[part, 2].wait_recv()
        send(part, 4, relay.at[part, 0], came.at[left, pl.ds(*low)], at_x(right))
        copies[part, 3].wait_recv()
        send(part, 5, relay.at[part, 1], came.at[right, pl.ds(*high)], at_x(left))

    def combine(part):
        for item in (0, 1, 4, 5):
            copies[part, item].wait_recv()
        lo = part * ROWS
        lines = [stats[x, :, lo : lo + ROWS]] + [
            came_stats[at, :, lo : lo + ROWS] for at in (right, left, far)
        ]
        shares = []
        for head in range(2):
            tops = [line[2 * head : 2 * head + 1] for line in lines]
            best = functools.reduce(jnp.maximum, tops)
            mass = [
                line[2 * head + 1 : 2 * head + 2] * jnp.exp(one - best)
                for line, one in zip(lines, tops)
            ]
            whole = jnp.maximum(sum(mass), 1e-30)
            shares += [one / whole for one in mass]
        turned = jnp.transpose(
            jnp.concatenate(shares + [jnp.zeros((120, ROWS), F32)], axis=0)
        )
        blocks = [part_out[x, lo : lo + ROWS, :]] + [
            came[at, lo : lo + ROWS, :] for at in (right, left, far)
        ]
        for head in range(2):
            mixed = sum(
                block[:, head * 128 : (head + 1) * 128].astype(F32)
                * turned[:, head * 4 + i : head * 4 + i + 1]
                for i, block in enumerate(blocks)
            ).astype(BF16)
            own[lo : lo + ROWS, head * 128 : (head + 1) * 128] = mixed
            held[tp, lo : lo + ROWS, head * 128 : (head + 1) * 128] = mixed

    def finish(lo):
        for part in range(lo // ROWS, (lo + DONE) // ROWS):
            gather.settle(part)
        total[...] = jnp.zeros_like(total)

        @pl.loop(0, TP)
        def _(slot):
            total[...] += jnp.dot(
                held[slot, lo : lo + DONE, :], weights[slot], preferred_element_type=F32
            )

        update[lo : lo + DONE, :] = (total[...] * gate[lo : lo + DONE, :1]).astype(BF16)

    def pass_on(part):
        combine(part)
        gather.begin(part)

    begin(0)
    middle(0)
    begin(1)
    for copy in told:
        copy.wait_recv()
    pass_on(0)
    middle(1)
    gather.middle(0)
    pass_on(1)
    gather.end(0)
    for load in loads:
        load.wait()
    gather.middle(1)
    finish(0)
    gather.end(1)
    finish(DONE)
    for copy in told + list(copies.values()):
        copy.wait_send()
    gather.drain()


def merge(part_out, stats, gate, columns):
    share, width = columns.shape[2:]
    dma = pltpu.SemaphoreType.DMA
    return pl.pallas_call(
        merge_kernel,
        out_shape=jax.ShapeDtypeStruct((SLOTS, width), BF16),
        in_specs=[VMEM, VMEM, VMEM, FAR],
        out_specs=VMEM,
        scratch_shapes=[
            pltpu.VMEM((NX, SLOTS, 256), BF16),
            pltpu.VMEM((NX, 8, SLOTS), F32),
            pltpu.VMEM((MERGES, 2, ROWS // 2, 256), BF16),
            pltpu.VMEM((SLOTS, 256), BF16),
            pltpu.VMEM((TP, SLOTS, 256), BF16),
            pltpu.VMEM((TP, NX * share, width), BF16),
            pltpu.VMEM((DONE, width), F32),
            dma((MERGES * 6,)), dma((MERGES * 6,)),
            dma((3,)), dma((3,)),
            dma((MERGES * 9,)), dma((MERGES * 9,)),
            dma((NX,)),
        ],
        compiler_params=pltpu.CompilerParams(
            collective_id=1, has_side_effects=True, vmem_limit_bytes=20 * MIB
        ),
        cost_estimate=pl.CostEstimate(flops=1 << 30, bytes_accessed=8 << 20, transcendentals=0),
        name="merge",
    )(part_out, stats, gate, columns)


WINDOW = 64


def spread_kernel(counts, tokens, rank, update, out):
    blocks = rank.shape[0]
    begin = pl.program_id(0) * blocks
    before = lax.fori_loop(0, begin, lambda b, sofar: sofar + counts[b], jnp.int32(0))
    turned = jnp.transpose(rank[...])
    slot = lax.broadcasted_iota(jnp.int32, (128, WINDOW), 1).astype(F32)
    for b in range(blocks):
        first = jnp.minimum(before // 16 * 16, SLOTS - WINDOW)
        place = jnp.where(turned[:, b : b + 1] - first.astype(F32) == slot, 1.0, 0.0).astype(BF16)
        near = update[pl.ds(pl.multiple_of(first, 16), WINDOW), :]
        added = jnp.dot(place, near, preferred_element_type=F32)
        rows = slice(b * 128, (b + 1) * 128)
        out[rows, :] = (tokens[rows, :].astype(F32) + added).astype(BF16)
        before = before + counts[begin + b]


def spread(counts, tokens, rank, update):
    tall, width = tokens.shape
    steps = rank.shape[0] // 8
    return pl.pallas_call(
        spread_kernel,
        out_shape=jax.ShapeDtypeStruct((tall, width), BF16),
        grid_spec=pltpu.PrefetchScalarGridSpec(
            num_scalar_prefetch=1,
            grid=(steps,),
            in_specs=[
                pl.BlockSpec((tall // steps, width), lambda i, c: (i, 0)),
                pl.BlockSpec((8, 128), lambda i, c: (i, 0)),
                pl.BlockSpec((SLOTS, width), lambda i, c: (0, 0)),
            ],
            out_specs=pl.BlockSpec((tall // steps, width), lambda i, c: (i, 0)),
        ),
        compiler_params=pltpu.CompilerParams(vmem_limit_bytes=12 * MIB),
        cost_estimate=pl.CostEstimate(flops=1 << 28, bytes_accessed=5 << 20, transcendentals=0),
        name="spread",
    )(counts, tokens, rank, update)


def body(tokens, block_counts, block_orders, w_router, w_query, w_key, w_value, w_out):
    far = [
        pltpu.with_memory_space_constraint(array, pltpu.HBM)
        for array in (tokens, block_counts, block_orders, w_router, w_query, w_key, w_value, w_out)
    ]
    query, pair, gate, columns, rank = project(*far)
    part_out, stats = attend(query, pair)
    update = merge(part_out, stats, gate, columns)
    return spread(block_counts, tokens, rank, update)


def solution(mesh):
    return jax.shard_map(
        body,
        mesh=mesh,
        in_specs=(
            P("ctx", "tp"),
            P("ctx"),
            P("ctx", None),
            P("tp"),
            P(None, "tp"),
            P(None, "tp"),
            P(None, "tp"),
            P("tp", None),
        ),
        out_specs=P("ctx", "tp"),
        check_vma=False,
    )
```

```python
import functools

import jax
import jax.numpy as jnp
from jax import lax
from jax.experimental import pallas as pl
from jax.experimental.pallas import tpu as pltpu
from jax.sharding import PartitionSpec as P

NX, NY, NZ = 4, 4, 8
TP = 2 * NY
SLOTS = 512
PICK = 32
HEAD = 16
EXT = HEAD + SLOTS
HD = 128
SLOT_SPANS = [(0, 128), (128, 128), (256, 128), (384, 128)]
SPANS = [(0, HEAD + 128)] + [(HEAD + at, size) for at, size in SLOT_SPANS[1:]]
PARTS = len(SPANS)
LARGEST = 128
MERGES = 2
ROWS = SLOTS // MERGES
DONE = 256
SCALE = HD ** (-0.5)
MESH = pl.DeviceIdType.MESH
F32, BF16 = jnp.float32, jnp.bfloat16
VMEM = pl.BlockSpec(memory_space=pltpu.VMEM)
FAR = pl.BlockSpec(memory_space=pltpu.HBM)
MIB = 1 << 20


def halves(start, size, unit=16):
    first = -(-(size // 2) // unit) * unit
    return (start, first), (start + first, size - first)


def remote(src, dst, sems, item, device):
    return pltpu.make_async_remote_copy(
        src_ref=src, dst_ref=dst, send_sem=sems[0].at[item], recv_sem=sems[1].at[item],
        device_id=device, device_id_type=MESH,
    )


def greet(partners):
    barrier = pltpu.get_barrier_semaphore()
    for device in partners:
        pl.semaphore_signal(barrier, inc=1, device_id=device, device_id_type=MESH)


def await_greetings(partners):
    pl.semaphore_wait(pltpu.get_barrier_semaphore(), len(partners))


def pick_rows(counts, tokens, orders, arrivals, rows, rank, pick, total):
    blocks = orders.shape[0]
    turned = jnp.transpose(orders[...].astype(F32))
    lane = lax.broadcasted_iota(jnp.int32, (PICK, 128), 1).astype(F32)
    slot = lax.broadcasted_iota(jnp.int32, (PICK, 128), 0)
    chosen = []
    for b in range(blocks):
        hit = (turned[:PICK, b : b + 1] == lane) & (slot < counts[b])
        chosen.append(jnp.sum(jnp.where(hit, 1.0, 0.0), axis=0, keepdims=True))
    upper = (
        lax.broadcasted_iota(jnp.int32, (128, 128), 0) < lax.broadcasted_iota(jnp.int32, (128, 128), 1)
    )
    chosen = jnp.concatenate(chosen, axis=0)
    within = jnp.dot(
        chosen.astype(BF16), jnp.where(upper, 1.0, 0.0).astype(BF16), preferred_element_type=F32
    )
    before = jnp.int32(0)
    index = lax.broadcasted_iota(jnp.int32, (SLOTS, 128), 0).astype(F32)
    for b in range(blocks):
        line = jnp.where(
            chosen[b : b + 1] > 0.5, within[b : b + 1] + before.astype(F32), -1.0
        )
        rank[b : b + 1, :] = line
        pick[:, b * 128 : (b + 1) * 128] = jnp.where(index == line, 1.0, 0.0).astype(BF16)
        before = before + counts[b]
    tall = tokens.shape[0] // len(arrivals)
    for at, copy in enumerate(arrivals):
        copy.wait()
        some = slice(at * tall, (at + 1) * tall)
        made = jnp.dot(pick[:, some], tokens[some, :], preferred_element_type=F32)
        if at == 0:
            total[...] = made
        elif at < len(arrivals) - 1:
            total[...] += made
        else:
            rows[...] = (total[...] + made).astype(BF16)
    return before


class TpGather:
    def __init__(self, own, held, sems, spans):
        tp, ctx = lax.axis_index("tp"), lax.axis_index("ctx")
        y, core = tp // 2, tp % 2
        self.own, self.held, self.sems, self.spans, self.tp = own, held, sems, spans, tp
        self.up_slot = ((y + 1) % NY) * 2 + core
        self.down_slot = ((y + NY - 1) % NY) * 2 + core
        self.far_slot = ((y + 2) % NY) * 2 + core
        self.up, self.down = (ctx, self.up_slot), (ctx, self.down_slot)
        self.sibling = (ctx, y * 2 + 1 - core)
        self.partners = [self.up, self.down, self.sibling]
        self.copies = {}

    def send(self, part, item, src, slot, rows, device):
        copy = remote(
            src.at[pl.ds(*rows)], self.held.at[slot, pl.ds(*rows)], self.sems, part * 9 + item, device
        )
        copy.start()
        self.copies[part, item] = copy

    def begin(self, part):
        rows = self.spans[part]
        self.send(part, 0, self.own, self.tp, rows, self.up)
        self.send(part, 1, self.own, self.tp, rows, self.down)
        self.send(part, 2, self.own, self.tp, rows, self.sibling)

    def middle(self, part):
        rows = self.spans[part]
        low, high = halves(*rows)
        self.copies[part, 0].wait_recv()
        self.send(part, 3, self.held.at[self.down_slot], self.down_slot, low, self.up)
        self.send(part, 5, self.held.at[self.down_slot], self.down_slot, rows, self.sibling)
        self.copies[part, 1].wait_recv()
        self.send(part, 4, self.held.at[self.up_slot], self.up_slot, high, self.down)
        self.send(part, 6, self.held.at[self.up_slot], self.up_slot, rows, self.sibling)

    def end(self, part):
        low, high = halves(*self.spans[part])
        self.copies[part, 3].wait_recv()
        self.send(part, 7, self.held.at[self.far_slot], self.far_slot, low, self.sibling)
        self.copies[part, 4].wait_recv()
        self.send(part, 8, self.held.at[self.far_slot], self.far_slot, high, self.sibling)

    def settle(self, part):
        for item in (2, 5, 6, 7, 8):
            self.copies[part, item].wait_recv()

    def drain(self):
        for copy in self.copies.values():
            copy.wait_send()


class RingGather:
    def __init__(self, held, sems, spans, me, size, device_of, unit=16):
        self.held, self.sems, self.spans, self.me, self.size = held, sems, spans, me, size
        self.up, self.down = device_of((me + 1) % size), device_of((me + size - 1) % size)
        self.partners = [self.up, self.down]
        self.unit = unit
        self.copies = {}

    def send(self, part, hop, way, slot, rows):
        item = hop * 2 + way
        at = self.held.at[slot, pl.ds(*rows)]
        copy = remote(at, at, self.sems, part * self.size + item, self.down if way else self.up)
        copy.start()
        self.copies[part, item] = copy

    def begin(self, part):
        self.send(part, 0, 0, self.me, self.spans[part])
        self.send(part, 0, 1, self.me, self.spans[part])

    def hop(self, part, hop):
        rows = self.spans[part]
        low, high = halves(*rows, self.unit)
        last = hop == self.size // 2 - 1
        self.copies[part, hop * 2 - 2].wait_recv()
        self.send(part, hop, 0, (self.me + self.size - hop) % self.size, low if last else rows)
        self.copies[part, hop * 2 - 1].wait_recv()
        self.send(part, hop, 1, (self.me + hop) % self.size, high if last else rows)

    def end(self, part):
        self.copies[part, self.size - 2].wait_recv()
        self.copies[part, self.size - 1].wait_recv()

    def drain(self):
        for copy in self.copies.values():
            copy.wait_send()


class Swap:
    def __init__(self, matrix, held, relay, sems, first):
        tp, ctx = lax.axis_index("tp"), lax.axis_index("ctx")
        self.y, self.core, self.tp, self.ctx = tp // 2, tp % 2, tp, ctx
        self.matrix, self.held, self.relay, self.sems = matrix, held, relay, sems
        self.depth, self.width = held.shape[1], held.shape[2]
        self.first = first
        self.copies = {}
        self.cores = [self.core, 1 - self.core]
        self.partners = [self.device(step, core) for step in (1, NY - 1) for core in self.cores]
        self.partners.append((ctx, self.y * 2 + 1 - self.core))

    def slot(self, step, core):
        return ((self.y + step) % NY) * 2 + core

    def device(self, step, core):
        return (self.ctx, self.slot(step, core))

    def block(self, slot, rows):
        start, size = rows
        rows = pl.ds(pl.multiple_of(self.first + start, 16), size)
        return self.matrix.at[rows, pl.ds(pl.multiple_of(slot * self.width, 512), self.width)]

    def send(self, item, src, dst, device):
        copy = remote(src, dst, self.sems, item, device)
        copy.start()
        self.copies[item] = copy

    def begin(self):
        whole, half = (0, self.depth), self.depth // 2
        sibling = self.y * 2 + 1 - self.core
        for way, step in enumerate((1, NY - 1)):
            for i, core in enumerate(self.cores):
                far = self.slot(2, core)
                self.send(
                    way * 2 + i, self.block(far, (way * half, half)), self.relay.at[way, i],
                    self.device(step, self.core),
                )
        for way, step in enumerate((1, NY - 1)):
            for i, core in enumerate(self.cores):
                self.send(
                    4 + way * 2 + i, self.block(self.slot(step, core), whole), self.held.at[self.tp],
                    self.device(step, core),
                )
        self.send(12, self.block(sibling, whole), self.held.at[self.tp], (self.ctx, sibling))

    def middle(self):
        half = self.depth // 2
        for way, step in enumerate((1, NY - 1)):
            source = self.slot(NY - step, self.core)
            for i, core in enumerate(self.cores):
                self.copies[way * 2 + i].wait_recv()
                self.send(
                    8 + way * 2 + i, self.relay.at[way, i],
                    self.held.at[source, pl.ds(way * half, half)], self.device(step, core),
                )

    def end(self):
        for item in range(4, 13):
            self.copies[item].wait_recv()

    def drain(self):
        for copy in self.copies.values():
            copy.wait_send()


def project_kernel(
    far_tokens, far_counts, far_orders, router, w_query, w_key, w_value, w_out,
    query, pair, gate, columns, rank,
    counts, tokens, orders, pick, gathered, held, weights, total, square, score, relay,
    a_send, a_recv, z_send, z_recv, x_send, x_recv, w_send, w_recv, c_send, c_recv, local_sem,
):
    ctx, tp = lax.axis_index("ctx"), lax.axis_index("tp")
    z, x = ctx // NX, ctx % NX
    depth, width = columns.shape[2:]
    inner = weights.shape[0] // TP
    tall = TpGather(held.at[tp], held, (a_send, a_recv), SPANS)
    pairs = RingGather(pair, (z_send, z_recv), SPANS, z, NZ, lambda at: (at * NX + x, tp))
    queries = RingGather(query, (x_send, x_recv), SPANS, x, NX, lambda at: (z * NX + at, tp))
    swap = Swap(w_out, columns.at[x], relay, (w_send, w_recv), x * depth)
    shares = RingGather(
        columns, (c_send, c_recv), [(0, TP)], x, NX, lambda at: (z * NX + at, tp), 1
    )

    partners = pairs.partners + queries.partners + swap.partners
    greet(partners)
    small = [
        pltpu.make_async_copy(far_counts, counts, local_sem.at[4]),
        pltpu.make_async_copy(far_orders, orders, local_sem.at[5]),
    ]
    quarter = tokens.shape[0] // 4
    large = [
        pltpu.make_async_copy(
            far_tokens.at[pl.ds(at * quarter, quarter)],
            tokens.at[pl.ds(at * quarter, quarter)],
            local_sem.at[6 + at],
        )
        for at in range(4)
    ]
    loads = [
        pltpu.make_async_copy(w_query, weights.at[:, pl.ds(0, 256)], local_sem.at[0]),
        pltpu.make_async_copy(w_key, weights.at[:, pl.ds(256, 128)], local_sem.at[1]),
        pltpu.make_async_copy(w_value, weights.at[:, pl.ds(384, 128)], local_sem.at[2]),
        pltpu.make_async_copy(
            w_out.at[
                pl.ds(pl.multiple_of(x * depth, 16), depth),
                pl.ds(pl.multiple_of(tp * width, 512), width),
            ],
            columns.at[x, tp],
            local_sem.at[3],
        ),
    ]
    for load in small + large + loads:
        load.start()
    for load in small:
        load.wait()
    held[tp, :HEAD, :] = jnp.broadcast_to(router[...].reshape(1, width), (HEAD, width))
    number = pick_rows(
        counts, tokens, orders, large, held.at[tp, pl.ds(HEAD, SLOTS)], rank, pick, gathered
    )
    high = number // 16
    for ref in (query.at[x], pair.at[z]):
        ref[:HEAD, :128] = jnp.full((HEAD, 128), high.astype(F32), F32).astype(BF16)
        ref[:HEAD, 128:] = jnp.full((HEAD, 128), (number - high * 16).astype(F32), F32).astype(BF16)
    await_greetings(partners)

    def project(part):
        start, size = SLOT_SPANS[part]
        start += HEAD
        here = slice(0, size)
        tall.settle(part)
        total[here, :] = jnp.zeros((size, 512), F32)
        square[here, :] = jnp.zeros((size, 128), F32)
        score[here, :] = jnp.zeros((size, 128), F32)

        @pl.loop(0, TP)
        def _(slot):
            block = held[slot, start : start + size, :]
            deep = pl.ds(pl.multiple_of(slot * inner, 512), inner)
            total[here, :] += jnp.dot(block, weights[deep, :], preferred_element_type=F32)
            router = held[slot, 0:HEAD, :].astype(F32)[0:1]
            wide = block.astype(F32)
            both, dots = wide * wide, wide * router
            square[here, :] += sum(both[:, c : c + 128] for c in range(0, inner, 128))
            score[here, :] += sum(dots[:, c : c + 128] for c in range(0, inner, 128))

        inv = lax.rsqrt(jnp.sum(square[here, :], axis=1, keepdims=True) / weights.shape[0] + 1e-05)
        open_ = jax.nn.sigmoid(jnp.sum(score[here, :], axis=1, keepdims=True))
        gate[start - HEAD : start - HEAD + size, :] = jnp.broadcast_to(open_, (size, 128))
        query[x, start : start + size, :] = (total[here, :256] * inv).astype(BF16)
        pair[z, start : start + size, :] = (total[here, 256:] * inv).astype(BF16)
        pairs.begin(part)
        queries.begin(part)

    tall.begin(0)
    tall.begin(1)
    tall.middle(0)
    tall.begin(2)
    tall.middle(1)
    swap.begin()
    tall.begin(3)
    tall.end(0)
    for load in loads:
        load.wait()
    project(0)
    tall.end(1)
    tall.middle(2)
    swap.middle()
    project(1)
    queries.hop(0, 1)
    pairs.hop(0, 1)
    tall.middle(3)
    queries.hop(1, 1)
    pairs.hop(1, 1)
    tall.end(2)
    pairs.hop(0, 2)
    swap.end()
    shares.begin(0)
    project(2)
    tall.end(3)
    pairs.hop(0, 3)
    pairs.hop(1, 2)
    project(3)
    pairs.hop(2, 1)
    pairs.hop(1, 3)
    pairs.hop(3, 1)
    pairs.hop(2, 2)
    shares.hop(0, 1)
    pairs.hop(3, 2)
    queries.hop(2, 1)
    pairs.hop(2, 3)
    queries.hop(3, 1)
    pairs.hop(3, 3)
    for part in range(PARTS):
        queries.end(part)
        pairs.end(part)
    shares.end(0)
    tall.drain()
    swap.drain()
    queries.drain()
    pairs.drain()
    shares.drain()


def project(tokens, counts, orders, router, w_query, w_key, w_value, w_out):
    tall, width = tokens.shape
    deep = w_query.shape[0]
    share = w_out.shape[0] // NX
    dma = pltpu.SemaphoreType.DMA
    return pl.pallas_call(
        project_kernel,
        out_shape=(
            jax.ShapeDtypeStruct((NX, EXT, 256), BF16),
            jax.ShapeDtypeStruct((NZ, EXT, 256), BF16),
            jax.ShapeDtypeStruct((SLOTS, 128), F32),
            jax.ShapeDtypeStruct((NX, TP, share, width), BF16),
            jax.ShapeDtypeStruct(orders.shape, F32),
        ),
        in_specs=[FAR, FAR, FAR, VMEM, FAR, FAR, FAR, FAR],
        out_specs=(VMEM, VMEM, VMEM, FAR, VMEM),
        scratch_shapes=[
            pltpu.SMEM(counts.shape, jnp.int32),
            pltpu.VMEM(tokens.shape, BF16),
            pltpu.VMEM(orders.shape, jnp.int32),
            pltpu.VMEM((SLOTS, tall), BF16),
            pltpu.VMEM((SLOTS, width), F32),
            pltpu.VMEM((TP, EXT, width), BF16),
            pltpu.VMEM((deep, 512), BF16),
            pltpu.VMEM((LARGEST, 512), F32),
            pltpu.VMEM((LARGEST, 128), F32),
            pltpu.VMEM((LARGEST, 128), F32),
            pltpu.VMEM((2, 2, share // 2, width), BF16),
            dma((PARTS * 9,)), dma((PARTS * 9,)),
            dma((PARTS * NZ,)), dma((PARTS * NZ,)),
            dma((PARTS * NX,)), dma((PARTS * NX,)),
            dma((13,)), dma((13,)),
            dma((NX,)), dma((NX,)),
            dma((10,)),
        ],
        compiler_params=pltpu.CompilerParams(
            collective_id=0, has_side_effects=True, vmem_limit_bytes=28 * MIB
        ),
        cost_estimate=pl.CostEstimate(flops=2 << 30, bytes_accessed=16 << 20, transcendentals=0),
        name="project",
    )(tokens, counts, orders, router, w_query, w_key, w_value, w_out)


KEYS = 1024
QROWS = 512


def attend_kernel(
    query, pair, out, stats, kp, vp, qp, op, sp, top, accum, first_scores, second_scores, table, numbers, sem
):
    ctx = lax.axis_index("ctx")
    z, x = ctx // NX, ctx % NX

    heads = [query[at, :HEAD, :] for at in range(NX)] + [pair[at, :HEAD, :] for at in range(NZ)]
    for at, head in enumerate(heads):
        head = head.astype(F32)[0:1]
        table[at : at + 1, :] = (head[:, :128] * 16.0 + head[:, 128:]).astype(jnp.int32)
    read = pltpu.make_async_copy(table, numbers, sem)
    read.start()

    def padded(n):
        return (n + 15) // 16 * 16

    slot = lax.broadcasted_iota(jnp.int32, (SLOTS, 128), 0)
    lane = lax.broadcasted_iota(jnp.int32, (SLOTS, 128), 1)
    op[...] = jnp.zeros_like(op)
    sp[...] = jnp.zeros_like(sp)
    read.wait()

    q_from = []
    used = jnp.int32(0)
    for at in range(NX):
        rows = pl.ds(pl.multiple_of(used, 16), SLOTS)
        for head in range(2):
            scaled = query[at, HEAD:, head * 128 : (head + 1) * 128].astype(F32) * SCALE
            high = scaled.astype(BF16)
            qp[head, rows, :128] = high
            qp[head, rows, 128:] = (scaled - high.astype(F32)).astype(BF16)
        q_from.append(used)
        used = used + padded(numbers[at, 0])
    q_blocks = (used + QROWS - 1) // QROWS

    def pack(at, place, n):
        rows = pl.ds(pl.multiple_of(place, 16), SLOTS)
        valid = slot < n
        keys = pair[at, HEAD:, :128]
        first = jnp.broadcast_to(keys[0:1].astype(F32), (SLOTS, 128)).astype(BF16)
        keys = jnp.where(valid, keys, first)
        kp[rows, :128] = keys
        kp[rows, 128:] = keys
        vp[rows, :128] = pair[at, HEAD:, 128:]
        vp[rows, 128:] = jnp.where(valid & (lane == 0), 1.0, 0.0).astype(BF16)

    here = numbers[NX + z, 0]
    pack(z, jnp.int32(0), here)

    def earlier(at, place):
        n = numbers[NX + at, 0]
        pack(at, place, n)
        return place + padded(n)

    last = lax.fori_loop(0, z, earlier, jnp.int32(SLOTS))
    first = jnp.broadcast_to(kp[SLOTS : SLOTS + 16, :][0:1].astype(F32), (KEYS, 256)).astype(BF16)
    rows = pl.ds(pl.multiple_of(last, 16), KEYS)
    kp[rows, :] = first
    vp[rows, :] = jnp.zeros((KEYS, 256), BF16)
    k_blocks = (last - SLOTS + KEYS - 1) // KEYS

    mine = jnp.int32(0)
    for at in range(NX):
        mine = jnp.where(x == at, q_from[at], mine)

    def score(head, q_rows, k_rows):
        return lax.dot_general(
            qp[head, q_rows, :], kp[k_rows, :], (((1,), (1,)), ((), ())), preferred_element_type=F32
        )

    def absorb(head, scores, k_rows, mask=None):
        spot = slice(head * QROWS, (head + 1) * QROWS)
        if mask is not None:
            scores = jnp.where(mask, scores, -1e30)
        old = top[spot, :]
        new = jnp.maximum(old, jnp.max(scores, axis=1, keepdims=True))
        shrink = jnp.exp(old - new)
        expo = jnp.exp(scores - new[:, :1])
        top[spot, :] = new
        made = jnp.dot(expo.astype(BF16), vp[k_rows, :], preferred_element_type=F32)
        accum[spot, :128] = accum[spot, :128] * shrink + made[:, :128]
        accum[spot, 128:] = accum[spot, 128:] * shrink + made[:, 128:]

    def k_at(step):
        return pl.ds(pl.multiple_of(SLOTS + step * KEYS, 512), KEYS)

    def q_block(at, carry):
        begin = at * QROWS
        q_rows = pl.ds(pl.multiple_of(begin, QROWS), QROWS)
        top[...] = jnp.full_like(top, -1e29)
        accum[...] = jnp.zeros_like(accum)

        @pl.when(begin + QROWS > mine)
        def _():
            row = begin + lax.broadcasted_iota(jnp.int32, (QROWS, SLOTS), 0)
            key = lax.broadcasted_iota(jnp.int32, (QROWS, SLOTS), 1)
            mask = key < jnp.clip(row - mine + 1, 0, here)
            own = pl.ds(0, SLOTS)
            first_scores[:, :SLOTS] = score(0, q_rows, own)
            second_scores[:, :SLOTS] = score(1, q_rows, own)
            absorb(0, first_scores[:, :SLOTS], own, mask)
            absorb(1, second_scores[:, :SLOTS], own, mask)

        @pl.when(k_blocks > 0)
        def _():
            first_scores[...] = score(0, q_rows, k_at(0))

        def k_block(step, carry):
            second_scores[...] = score(1, q_rows, k_at(step))
            absorb(0, first_scores[...], k_at(step))
            first_scores[...] = score(0, q_rows, k_at(jnp.minimum(step + 1, k_blocks - 1)))
            absorb(1, second_scores[...], k_at(step))
            return carry

        lax.fori_loop(0, k_blocks, k_block, 0)
        spot = lax.broadcasted_iota(jnp.int32, (QROWS, 128), 1)
        kept = jnp.zeros((QROWS, 128), F32)
        for head in range(2):
            part = slice(head * QROWS, (head + 1) * QROWS)
            whole = accum[part, 128:129]
            op[q_rows, head * 128 : (head + 1) * 128] = (
                accum[part, :128] / jnp.maximum(whole, 1e-30)
            ).astype(BF16)
            kept = jnp.where(spot == 2 * head, top[part, :], kept)
            kept = jnp.where(spot == 2 * head + 1, whole, kept)
        sp[q_rows, :] = kept
        return carry

    lax.fori_loop(0, q_blocks, q_block, 0)
    for at in range(NX):
        rows = pl.ds(pl.multiple_of(q_from[at], 16), SLOTS)
        out[at] = op[rows, :]
        stats[at] = jnp.transpose(sp[rows, :])[:8]


def attend(query, pair):
    packed_q = (NX + 1) * SLOTS
    packed_k = (NZ + 1) * SLOTS + KEYS
    return pl.pallas_call(
        attend_kernel,
        out_shape=(
            jax.ShapeDtypeStruct((NX, SLOTS, 256), BF16),
            jax.ShapeDtypeStruct((NX, 8, SLOTS), F32),
        ),
        in_specs=[VMEM, VMEM],
        out_specs=(VMEM, VMEM),
        scratch_shapes=[
            pltpu.VMEM((packed_k, 256), BF16),
            pltpu.VMEM((packed_k, 256), BF16),
            pltpu.VMEM((2, packed_q, 256), BF16),
            pltpu.VMEM((packed_q, 256), BF16),
            pltpu.VMEM((packed_q, 128), F32),
            pltpu.VMEM((2 * QROWS, 128), F32),
            pltpu.VMEM((2 * QROWS, 256), F32),
            pltpu.VMEM((QROWS, KEYS), F32),
            pltpu.VMEM((QROWS, KEYS), F32),
            pltpu.VMEM((16, 128), jnp.int32),
            pltpu.SMEM((16, 128), jnp.int32),
            pltpu.SemaphoreType.DMA,
        ],
        compiler_params=pltpu.CompilerParams(vmem_limit_bytes=28 * MIB),
        cost_estimate=pl.CostEstimate(flops=4 << 30, bytes_accessed=8 << 20, transcendentals=4 << 20),
        name="attend",
    )(query, pair)


def merge_kernel(
    part_out, stats, gate, columns, update,
    came, came_stats, relay, own, held, weights, total,
    x_send, x_recv, s_send, s_recv, a_send, a_recv, local_sem,
):
    ctx, tp = lax.axis_index("ctx"), lax.axis_index("tp")
    z, x = ctx // NX, ctx % NX
    right, left, far = (x + 1) % NX, (x + NX - 1) % NX, (x + 2) % NX

    def at_x(at):
        return (z * NX + at, tp)

    spans = [(part * ROWS, ROWS) for part in range(MERGES)]
    gather = TpGather(own, held, (a_send, a_recv), spans)
    share = columns.shape[2]
    loads = [
        pltpu.make_async_copy(columns.at[at], weights.at[:, pl.ds(at * share, share)], local_sem.at[at])
        for at in range(NX)
    ]
    for load in loads:
        load.start()
    partners = gather.partners + [at_x(right), at_x(left), at_x(far)]
    greet(partners)
    await_greetings(partners)

    copies = {}

    def send(part, item, src, dst, device):
        copy = remote(src, dst, (x_send, x_recv), part * 6 + item, device)
        copy.start()
        copies[part, item] = copy

    told = []
    for item, to in enumerate((right, left, far)):
        copy = remote(stats.at[to], came_stats.at[x], (s_send, s_recv), item, at_x(to))
        copy.start()
        told.append(copy)

    def begin(part):
        rows = spans[part]
        low, high = halves(*rows)
        send(part, 2, part_out.at[far, pl.ds(*low)], relay.at[part, 0], at_x(right))
        send(part, 3, part_out.at[far, pl.ds(*high)], relay.at[part, 1], at_x(left))
        send(part, 0, part_out.at[right, pl.ds(*rows)], came.at[x, pl.ds(*rows)], at_x(right))
        send(part, 1, part_out.at[left, pl.ds(*rows)], came.at[x, pl.ds(*rows)], at_x(left))

    def middle(part):
        low, high = halves(*spans[part])
        copies[part, 2].wait_recv()
        send(part, 4, relay.at[part, 0], came.at[left, pl.ds(*low)], at_x(right))
        copies[part, 3].wait_recv()
        send(part, 5, relay.at[part, 1], came.at[right, pl.ds(*high)], at_x(left))

    def combine(part):
        for item in (0, 1, 4, 5):
            copies[part, item].wait_recv()
        lo = part * ROWS
        lines = [stats[x, :, lo : lo + ROWS]] + [
            came_stats[at, :, lo : lo + ROWS] for at in (right, left, far)
        ]
        shares = []
        for head in range(2):
            tops = [line[2 * head : 2 * head + 1] for line in lines]
            best = functools.reduce(jnp.maximum, tops)
            mass = [
                line[2 * head + 1 : 2 * head + 2] * jnp.exp(one - best)
                for line, one in zip(lines, tops)
            ]
            whole = jnp.maximum(sum(mass), 1e-30)
            shares += [one / whole for one in mass]
        turned = jnp.transpose(
            jnp.concatenate(shares + [jnp.zeros((120, ROWS), F32)], axis=0)
        )
        blocks = [part_out[x, lo : lo + ROWS, :]] + [
            came[at, lo : lo + ROWS, :] for at in (right, left, far)
        ]
        for head in range(2):
            mixed = sum(
                block[:, head * 128 : (head + 1) * 128].astype(F32)
                * turned[:, head * 4 + i : head * 4 + i + 1]
                for i, block in enumerate(blocks)
            ).astype(BF16)
            own[lo : lo + ROWS, head * 128 : (head + 1) * 128] = mixed
            held[tp, lo : lo + ROWS, head * 128 : (head + 1) * 128] = mixed

    def finish(lo):
        for part in range(lo // ROWS, (lo + DONE) // ROWS):
            gather.settle(part)
        total[...] = jnp.zeros_like(total)

        @pl.loop(0, TP)
        def _(slot):
            total[...] += jnp.dot(
                held[slot, lo : lo + DONE, :], weights[slot], preferred_element_type=F32
            )

        update[lo : lo + DONE, :] = (total[...] * gate[lo : lo + DONE, :1]).astype(BF16)

    def pass_on(part):
        combine(part)
        gather.begin(part)

    begin(0)
    middle(0)
    begin(1)
    for copy in told:
        copy.wait_recv()
    pass_on(0)
    middle(1)
    gather.middle(0)
    pass_on(1)
    gather.end(0)
    for load in loads:
        load.wait()
    gather.middle(1)
    finish(0)
    gather.end(1)
    finish(DONE)
    for copy in told + list(copies.values()):
        copy.wait_send()
    gather.drain()


def merge(part_out, stats, gate, columns):
    share, width = columns.shape[2:]
    dma = pltpu.SemaphoreType.DMA
    return pl.pallas_call(
        merge_kernel,
        out_shape=jax.ShapeDtypeStruct((SLOTS, width), BF16),
        in_specs=[VMEM, VMEM, VMEM, FAR],
        out_specs=VMEM,
        scratch_shapes=[
            pltpu.VMEM((NX, SLOTS, 256), BF16),
            pltpu.VMEM((NX, 8, SLOTS), F32),
            pltpu.VMEM((MERGES, 2, ROWS // 2, 256), BF16),
            pltpu.VMEM((SLOTS, 256), BF16),
            pltpu.VMEM((TP, SLOTS, 256), BF16),
            pltpu.VMEM((TP, NX * share, width), BF16),
            pltpu.VMEM((DONE, width), F32),
            dma((MERGES * 6,)), dma((MERGES * 6,)),
            dma((3,)), dma((3,)),
            dma((MERGES * 9,)), dma((MERGES * 9,)),
            dma((NX,)),
        ],
        compiler_params=pltpu.CompilerParams(
            collective_id=1, has_side_effects=True, vmem_limit_bytes=20 * MIB
        ),
        cost_estimate=pl.CostEstimate(flops=1 << 30, bytes_accessed=8 << 20, transcendentals=0),
        name="merge",
    )(part_out, stats, gate, columns)


WINDOW = 64


def spread_kernel(counts, tokens, rank, update, out, made, sems):
    blocks = rank.shape[0]
    turned = jnp.transpose(rank[...])
    slot = lax.broadcasted_iota(jnp.int32, (128, WINDOW), 1).astype(F32)
    before = jnp.int32(0)
    copies = []
    for b in range(blocks):
        first = jnp.minimum(before // 16 * 16, SLOTS - WINDOW)
        place = jnp.where(turned[:, b : b + 1] - first.astype(F32) == slot, 1.0, 0.0).astype(BF16)
        near = update[pl.ds(pl.multiple_of(first, 16), WINDOW), :]
        added = jnp.dot(place, near, preferred_element_type=F32)
        rows = slice(b * 128, (b + 1) * 128)
        made[rows, :] = (tokens[rows, :].astype(F32) + added).astype(BF16)
        before = before + counts[b]
        if b % 4 == 3:
            rows = pl.ds((b - 3) * 128, 512)
            copies.append(pltpu.make_async_copy(made.at[rows], out.at[rows], sems.at[b // 4]))
            copies[-1].start()
    for copy in copies:
        copy.wait()


def spread(counts, tokens, rank, update):
    return pl.pallas_call(
        spread_kernel,
        out_shape=jax.ShapeDtypeStruct(tokens.shape, BF16),
        in_specs=[pl.BlockSpec(memory_space=pltpu.SMEM), VMEM, VMEM, VMEM],
        out_specs=FAR,
        scratch_shapes=[
            pltpu.VMEM(tokens.shape, BF16),
            pltpu.SemaphoreType.DMA((rank.shape[0] // 4,)),
        ],
        compiler_params=pltpu.CompilerParams(vmem_limit_bytes=12 * MIB),
        cost_estimate=pl.CostEstimate(flops=1 << 28, bytes_accessed=5 << 20, transcendentals=0),
        name="spread",
    )(counts, tokens, rank, update)


def body(tokens, block_counts, block_orders, w_router, w_query, w_key, w_value, w_out):
    far = [
        pltpu.with_memory_space_constraint(array, pltpu.HBM)
        for array in (tokens, block_counts, block_orders, w_router, w_query, w_key, w_value, w_out)
    ]
    query, pair, gate, columns, rank = project(*far)
    part_out, stats = attend(query, pair)
    update = merge(part_out, stats, gate, columns)
    return spread(block_counts, tokens, rank, update)


def solution(mesh):
    return jax.shard_map(
        body,
        mesh=mesh,
        in_specs=(
            P("ctx", "tp"),
            P("ctx"),
            P("ctx", None),
            P("tp"),
            P(None, "tp"),
            P(None, "tp"),
            P(None, "tp"),
            P("tp", None),
        ),
        out_specs=P("ctx", "tp"),
        check_vma=False,
    )
```

```python
import functools

import jax
import jax.numpy as jnp
from jax import lax
from jax.experimental import pallas as pl
from jax.experimental.pallas import tpu as pltpu
from jax.sharding import PartitionSpec as P

NX, NY, NZ = 4, 4, 8
TP = 2 * NY
SLOTS = 512
PICK = 32
HEAD = 16
EXT = HEAD + SLOTS
HD = 128
SLOT_SPANS = [(0, 128), (128, 128), (256, 128), (384, 128)]
SPANS = [(0, HEAD + 128)] + [(HEAD + at, size) for at, size in SLOT_SPANS[1:]]
PARTS = len(SPANS)
LARGEST = 128
MERGES = 2
ROWS = SLOTS // MERGES
DONE = 256
SCALE = HD ** (-0.5)
MESH = pl.DeviceIdType.MESH
F32, BF16 = jnp.float32, jnp.bfloat16
VMEM = pl.BlockSpec(memory_space=pltpu.VMEM)
FAR = pl.BlockSpec(memory_space=pltpu.HBM)
MIB = 1 << 20


def halves(start, size, unit=16):
    first = -(-(size // 2) // unit) * unit
    return (start, first), (start + first, size - first)


def remote(src, dst, sems, item, device):
    return pltpu.make_async_remote_copy(
        src_ref=src, dst_ref=dst, send_sem=sems[0].at[item], recv_sem=sems[1].at[item],
        device_id=device, device_id_type=MESH,
    )


def greet(partners):
    barrier = pltpu.get_barrier_semaphore()
    for device in partners:
        pl.semaphore_signal(barrier, inc=1, device_id=device, device_id_type=MESH)


def await_greetings(partners):
    pl.semaphore_wait(pltpu.get_barrier_semaphore(), len(partners))


def pick_rows(counts, tokens, orders, arrivals, rows, rank, pick, total):
    blocks = orders.shape[0]
    turned = jnp.transpose(orders[...].astype(F32))
    lane = lax.broadcasted_iota(jnp.int32, (PICK, 128), 1).astype(F32)
    slot = lax.broadcasted_iota(jnp.int32, (PICK, 128), 0)
    chosen = []
    for b in range(blocks):
        hit = (turned[:PICK, b : b + 1] == lane) & (slot < counts[b])
        chosen.append(jnp.sum(jnp.where(hit, 1.0, 0.0), axis=0, keepdims=True))
    upper = (
        lax.broadcasted_iota(jnp.int32, (128, 128), 0) < lax.broadcasted_iota(jnp.int32, (128, 128), 1)
    )
    chosen = jnp.concatenate(chosen, axis=0)
    within = jnp.dot(
        chosen.astype(BF16), jnp.where(upper, 1.0, 0.0).astype(BF16), preferred_element_type=F32
    )
    before = jnp.int32(0)
    index = lax.broadcasted_iota(jnp.int32, (SLOTS, 128), 0).astype(F32)
    for b in range(blocks):
        line = jnp.where(
            chosen[b : b + 1] > 0.5, within[b : b + 1] + before.astype(F32), -1.0
        )
        rank[b : b + 1, :] = line
        pick[:, b * 128 : (b + 1) * 128] = jnp.where(index == line, 1.0, 0.0).astype(BF16)
        before = before + counts[b]
    tall = tokens.shape[0] // len(arrivals)
    for at, copy in enumerate(arrivals):
        copy.wait()
        some = slice(at * tall, (at + 1) * tall)
        made = jnp.dot(pick[:, some], tokens[some, :], preferred_element_type=F32)
        if at == 0:
            total[...] = made
        elif at < len(arrivals) - 1:
            total[...] += made
        else:
            rows[...] = (total[...] + made).astype(BF16)
    return before


class TpGather:
    def __init__(self, own, held, sems, spans):
        tp, ctx = lax.axis_index("tp"), lax.axis_index("ctx")
        y, core = tp // 2, tp % 2
        self.own, self.held, self.sems, self.spans, self.tp = own, held, sems, spans, tp
        self.up_slot = ((y + 1) % NY) * 2 + core
        self.down_slot = ((y + NY - 1) % NY) * 2 + core
        self.far_slot = ((y + 2) % NY) * 2 + core
        self.up, self.down = (ctx, self.up_slot), (ctx, self.down_slot)
        self.sibling = (ctx, y * 2 + 1 - core)
        self.partners = [self.up, self.down, self.sibling]
        self.copies = {}

    def send(self, part, item, src, slot, rows, device):
        copy = remote(
            src.at[pl.ds(*rows)], self.held.at[slot, pl.ds(*rows)], self.sems, part * 9 + item, device
        )
        copy.start()
        self.copies[part, item] = copy

    def begin(self, part):
        rows = self.spans[part]
        self.send(part, 0, self.own, self.tp, rows, self.up)
        self.send(part, 1, self.own, self.tp, rows, self.down)
        self.send(part, 2, self.own, self.tp, rows, self.sibling)

    def middle(self, part):
        rows = self.spans[part]
        low, high = halves(*rows)
        self.copies[part, 0].wait_recv()
        self.send(part, 3, self.held.at[self.down_slot], self.down_slot, low, self.up)
        self.send(part, 5, self.held.at[self.down_slot], self.down_slot, rows, self.sibling)
        self.copies[part, 1].wait_recv()
        self.send(part, 4, self.held.at[self.up_slot], self.up_slot, high, self.down)
        self.send(part, 6, self.held.at[self.up_slot], self.up_slot, rows, self.sibling)

    def end(self, part):
        low, high = halves(*self.spans[part])
        self.copies[part, 3].wait_recv()
        self.send(part, 7, self.held.at[self.far_slot], self.far_slot, low, self.sibling)
        self.copies[part, 4].wait_recv()
        self.send(part, 8, self.held.at[self.far_slot], self.far_slot, high, self.sibling)

    def settle(self, part):
        for item in (2, 5, 6, 7, 8):
            self.copies[part, item].wait_recv()

    def drain(self):
        for copy in self.copies.values():
            copy.wait_send()


class RingGather:
    def __init__(self, held, sems, spans, me, size, device_of, unit=16):
        self.held, self.sems, self.spans, self.me, self.size = held, sems, spans, me, size
        self.up, self.down = device_of((me + 1) % size), device_of((me + size - 1) % size)
        self.partners = [self.up, self.down]
        self.unit = unit
        self.copies = {}

    def send(self, part, hop, way, slot, rows):
        item = hop * 2 + way
        at = self.held.at[slot, pl.ds(*rows)]
        copy = remote(at, at, self.sems, part * self.size + item, self.down if way else self.up)
        copy.start()
        self.copies[part, item] = copy

    def begin(self, part):
        self.send(part, 0, 0, self.me, self.spans[part])
        self.send(part, 0, 1, self.me, self.spans[part])

    def hop(self, part, hop):
        rows = self.spans[part]
        low, high = halves(*rows, self.unit)
        last = hop == self.size // 2 - 1
        self.copies[part, hop * 2 - 2].wait_recv()
        self.send(part, hop, 0, (self.me + self.size - hop) % self.size, low if last else rows)
        self.copies[part, hop * 2 - 1].wait_recv()
        self.send(part, hop, 1, (self.me + hop) % self.size, high if last else rows)

    def end(self, part):
        self.copies[part, self.size - 2].wait_recv()
        self.copies[part, self.size - 1].wait_recv()

    def drain(self):
        for copy in self.copies.values():
            copy.wait_send()


class Swap:
    def __init__(self, matrix, held, relay, sems, first):
        tp, ctx = lax.axis_index("tp"), lax.axis_index("ctx")
        self.y, self.core, self.tp, self.ctx = tp // 2, tp % 2, tp, ctx
        self.matrix, self.held, self.relay, self.sems = matrix, held, relay, sems
        self.depth, self.width = held.shape[1], held.shape[2]
        self.first = first
        self.copies = {}
        self.cores = [self.core, 1 - self.core]
        self.partners = [self.device(step, core) for step in (1, NY - 1) for core in self.cores]
        self.partners.append((ctx, self.y * 2 + 1 - self.core))

    def slot(self, step, core):
        return ((self.y + step) % NY) * 2 + core

    def device(self, step, core):
        return (self.ctx, self.slot(step, core))

    def block(self, slot, rows):
        start, size = rows
        rows = pl.ds(pl.multiple_of(self.first + start, 16), size)
        return self.matrix.at[rows, pl.ds(pl.multiple_of(slot * self.width, 512), self.width)]

    def send(self, item, src, dst, device):
        copy = remote(src, dst, self.sems, item, device)
        copy.start()
        self.copies[item] = copy

    def begin(self):
        whole, half = (0, self.depth), self.depth // 2
        sibling = self.y * 2 + 1 - self.core
        for way, step in enumerate((1, NY - 1)):
            for i, core in enumerate(self.cores):
                far = self.slot(2, core)
                self.send(
                    way * 2 + i, self.block(far, (way * half, half)), self.relay.at[way, i],
                    self.device(step, self.core),
                )
        for way, step in enumerate((1, NY - 1)):
            for i, core in enumerate(self.cores):
                self.send(
                    4 + way * 2 + i, self.block(self.slot(step, core), whole), self.held.at[self.tp],
                    self.device(step, core),
                )
        self.send(12, self.block(sibling, whole), self.held.at[self.tp], (self.ctx, sibling))

    def middle(self):
        half = self.depth // 2
        for way, step in enumerate((1, NY - 1)):
            source = self.slot(NY - step, self.core)
            for i, core in enumerate(self.cores):
                self.copies[way * 2 + i].wait_recv()
                self.send(
                    8 + way * 2 + i, self.relay.at[way, i],
                    self.held.at[source, pl.ds(way * half, half)], self.device(step, core),
                )

    def end(self):
        for item in range(4, 13):
            self.copies[item].wait_recv()

    def drain(self):
        for copy in self.copies.values():
            copy.wait_send()


def project_kernel(
    far_tokens, far_counts, far_orders, router, w_query, w_key, w_value, w_out,
    query, pair, gate, columns, rank,
    counts, tokens, orders, pick, gathered, held, weights, total, square, score, relay,
    a_send, a_recv, z_send, z_recv, x_send, x_recv, w_send, w_recv, c_send, c_recv, local_sem,
):
    ctx, tp = lax.axis_index("ctx"), lax.axis_index("tp")
    z, x = ctx // NX, ctx % NX
    depth, width = columns.shape[2:]
    inner = weights.shape[0] // TP
    tall = TpGather(held.at[tp], held, (a_send, a_recv), SPANS)
    pairs = RingGather(pair, (z_send, z_recv), SPANS, z, NZ, lambda at: (at * NX + x, tp))
    queries = RingGather(query, (x_send, x_recv), SPANS, x, NX, lambda at: (z * NX + at, tp))
    swap = Swap(w_out, columns.at[x], relay, (w_send, w_recv), x * depth)
    shares = RingGather(
        columns, (c_send, c_recv), [(0, TP)], x, NX, lambda at: (z * NX + at, tp), 1
    )

    partners = pairs.partners + queries.partners + swap.partners
    greet(partners)
    small = [
        pltpu.make_async_copy(far_counts, counts, local_sem.at[4]),
        pltpu.make_async_copy(far_orders, orders, local_sem.at[5]),
    ]
    quarter = tokens.shape[0] // 4
    large = [
        pltpu.make_async_copy(
            far_tokens.at[pl.ds(at * quarter, quarter)],
            tokens.at[pl.ds(at * quarter, quarter)],
            local_sem.at[6 + at],
        )
        for at in range(4)
    ]
    loads = [
        pltpu.make_async_copy(w_query, weights.at[:, pl.ds(0, 256)], local_sem.at[0]),
        pltpu.make_async_copy(w_key, weights.at[:, pl.ds(256, 128)], local_sem.at[1]),
        pltpu.make_async_copy(w_value, weights.at[:, pl.ds(384, 128)], local_sem.at[2]),
        pltpu.make_async_copy(
            w_out.at[
                pl.ds(pl.multiple_of(x * depth, 16), depth),
                pl.ds(pl.multiple_of(tp * width, 512), width),
            ],
            columns.at[x, tp],
            local_sem.at[3],
        ),
    ]
    for load in small + large + loads:
        load.start()
    for load in small:
        load.wait()
    held[tp, :HEAD, :] = jnp.broadcast_to(router[...].reshape(1, width), (HEAD, width))
    number = pick_rows(
        counts, tokens, orders, large, held.at[tp, pl.ds(HEAD, SLOTS)], rank, pick, gathered
    )
    high = number // 16
    for ref in (query.at[x], pair.at[z]):
        ref[:HEAD, :128] = jnp.full((HEAD, 128), high.astype(F32), F32).astype(BF16)
        ref[:HEAD, 128:] = jnp.full((HEAD, 128), (number - high * 16).astype(F32), F32).astype(BF16)
    await_greetings(partners)

    def project(part):
        start, size = SLOT_SPANS[part]
        start += HEAD
        here = slice(0, size)
        tall.settle(part)
        total[here, :] = jnp.zeros((size, 512), F32)
        square[here, :] = jnp.zeros((size, 128), F32)
        score[here, :] = jnp.zeros((size, 128), F32)

        @pl.loop(0, TP)
        def _(slot):
            block = held[slot, start : start + size, :]
            deep = pl.ds(pl.multiple_of(slot * inner, 512), inner)
            total[here, :] += jnp.dot(block, weights[deep, :], preferred_element_type=F32)
            router = held[slot, 0:HEAD, :].astype(F32)[0:1]
            wide = block.astype(F32)
            both, dots = wide * wide, wide * router
            square[here, :] += sum(both[:, c : c + 128] for c in range(0, inner, 128))
            score[here, :] += sum(dots[:, c : c + 128] for c in range(0, inner, 128))

        inv = lax.rsqrt(jnp.sum(square[here, :], axis=1, keepdims=True) / weights.shape[0] + 1e-05)
        open_ = jax.nn.sigmoid(jnp.sum(score[here, :], axis=1, keepdims=True))
        gate[start - HEAD : start - HEAD + size, :] = jnp.broadcast_to(open_, (size, 128))
        query[x, start : start + size, :] = (total[here, :256] * inv).astype(BF16)
        pair[z, start : start + size, :] = (total[here, 256:] * inv).astype(BF16)
        pairs.begin(part)
        queries.begin(part)

    tall.begin(0)
    tall.begin(1)
    tall.middle(0)
    tall.begin(2)
    tall.middle(1)
    swap.begin()
    tall.begin(3)
    tall.end(0)
    for load in loads:
        load.wait()
    project(0)
    tall.end(1)
    tall.middle(2)
    swap.middle()
    project(1)
    queries.hop(0, 1)
    pairs.hop(0, 1)
    tall.middle(3)
    queries.hop(1, 1)
    pairs.hop(1, 1)
    tall.end(2)
    pairs.hop(0, 2)
    swap.end()
    shares.begin(0)
    project(2)
    tall.end(3)
    pairs.hop(0, 3)
    pairs.hop(1, 2)
    project(3)
    pairs.hop(2, 1)
    pairs.hop(1, 3)
    pairs.hop(3, 1)
    pairs.hop(2, 2)
    shares.hop(0, 1)
    pairs.hop(3, 2)
    queries.hop(2, 1)
    pairs.hop(2, 3)
    queries.hop(3, 1)
    pairs.hop(3, 3)
    for part in range(PARTS):
        queries.end(part)
        pairs.end(part)
    shares.end(0)
    tall.drain()
    swap.drain()
    queries.drain()
    pairs.drain()
    shares.drain()


def project(tokens, counts, orders, router, w_query, w_key, w_value, w_out):
    tall, width = tokens.shape
    deep = w_query.shape[0]
    share = w_out.shape[0] // NX
    dma = pltpu.SemaphoreType.DMA
    return pl.pallas_call(
        project_kernel,
        out_shape=(
            jax.ShapeDtypeStruct((NX, EXT, 256), BF16),
            jax.ShapeDtypeStruct((NZ, EXT, 256), BF16),
            jax.ShapeDtypeStruct((SLOTS, 128), F32),
            jax.ShapeDtypeStruct((NX, TP, share, width), BF16),
            jax.ShapeDtypeStruct(orders.shape, F32),
        ),
        in_specs=[FAR, FAR, FAR, VMEM, FAR, FAR, FAR, FAR],
        out_specs=(VMEM, VMEM, VMEM, FAR, VMEM),
        scratch_shapes=[
            pltpu.SMEM(counts.shape, jnp.int32),
            pltpu.VMEM(tokens.shape, BF16),
            pltpu.VMEM(orders.shape, jnp.int32),
            pltpu.VMEM((SLOTS, tall), BF16),
            pltpu.VMEM((SLOTS, width), F32),
            pltpu.VMEM((TP, EXT, width), BF16),
            pltpu.VMEM((deep, 512), BF16),
            pltpu.VMEM((LARGEST, 512), F32),
            pltpu.VMEM((LARGEST, 128), F32),
            pltpu.VMEM((LARGEST, 128), F32),
            pltpu.VMEM((2, 2, share // 2, width), BF16),
            dma((PARTS * 9,)), dma((PARTS * 9,)),
            dma((PARTS * NZ,)), dma((PARTS * NZ,)),
            dma((PARTS * NX,)), dma((PARTS * NX,)),
            dma((13,)), dma((13,)),
            dma((NX,)), dma((NX,)),
            dma((10,)),
        ],
        compiler_params=pltpu.CompilerParams(
            collective_id=0, has_side_effects=True, vmem_limit_bytes=28 * MIB
        ),
        cost_estimate=pl.CostEstimate(flops=2 << 30, bytes_accessed=16 << 20, transcendentals=0),
        name="project",
    )(tokens, counts, orders, router, w_query, w_key, w_value, w_out)


KEYS = 1024
QROWS = 512


def attend_kernel(
    query, pair, out, stats, kp, vp, qp, op, sp, top, accum, first_scores, second_scores, table, numbers, sem
):
    ctx = lax.axis_index("ctx")
    z, x = ctx // NX, ctx % NX

    heads = [query[at, :HEAD, :] for at in range(NX)] + [pair[at, :HEAD, :] for at in range(NZ)]
    for at, head in enumerate(heads):
        head = head.astype(F32)[0:1]
        table[at : at + 1, :] = (head[:, :128] * 16.0 + head[:, 128:]).astype(jnp.int32)
    read = pltpu.make_async_copy(table, numbers, sem)
    read.start()

    def padded(n):
        return (n + 15) // 16 * 16

    slot = lax.broadcasted_iota(jnp.int32, (SLOTS, 128), 0)
    lane = lax.broadcasted_iota(jnp.int32, (SLOTS, 128), 1)
    op[...] = jnp.zeros_like(op)
    sp[...] = jnp.zeros_like(sp)
    read.wait()

    q_from = []
    used = jnp.int32(0)
    for at in range(NX):
        rows = pl.ds(pl.multiple_of(used, 16), SLOTS)
        for head in range(2):
            scaled = query[at, HEAD:, head * 128 : (head + 1) * 128].astype(F32) * SCALE
            high = scaled.astype(BF16)
            qp[head, rows, :128] = high
            qp[head, rows, 128:] = (scaled - high.astype(F32)).astype(BF16)
        q_from.append(used)
        used = used + padded(numbers[at, 0])
    q_blocks = (used + QROWS - 1) // QROWS

    def pack(at, place, n):
        rows = pl.ds(pl.multiple_of(place, 16), SLOTS)
        valid = slot < n
        keys = pair[at, HEAD:, :128]
        first = jnp.broadcast_to(keys[0:1].astype(F32), (SLOTS, 128)).astype(BF16)
        keys = jnp.where(valid, keys, first)
        kp[rows, :128] = keys
        kp[rows, 128:] = keys
        vp[rows, :128] = pair[at, HEAD:, 128:]
        vp[rows, 128:] = jnp.where(valid & (lane == 0), 1.0, 0.0).astype(BF16)

    here = numbers[NX + z, 0]
    pack(z, jnp.int32(0), here)

    def earlier(at, place):
        n = numbers[NX + at, 0]
        pack(at, place, n)
        return place + padded(n)

    last = lax.fori_loop(0, z, earlier, jnp.int32(SLOTS))
    first = jnp.broadcast_to(kp[SLOTS : SLOTS + 16, :][0:1].astype(F32), (KEYS, 256)).astype(BF16)
    rows = pl.ds(pl.multiple_of(last, 16), KEYS)
    kp[rows, :] = first
    vp[rows, :] = jnp.zeros((KEYS, 256), BF16)
    k_halves = (last - SLOTS + KEYS // 2 - 1) // (KEYS // 2)
    k_blocks, k_half = k_halves // 2, k_halves % 2

    mine = jnp.int32(0)
    for at in range(NX):
        mine = jnp.where(x == at, q_from[at], mine)

    def score(head, q_rows, k_rows):
        return lax.dot_general(
            qp[head, q_rows, :], kp[k_rows, :], (((1,), (1,)), ((), ())), preferred_element_type=F32
        )

    def absorb(head, scores, k_rows, mask=None):
        spot = slice(head * QROWS, (head + 1) * QROWS)
        if mask is not None:
            scores = jnp.where(mask, scores, -1e30)
        old = top[spot, :]
        new = jnp.maximum(old, jnp.max(scores, axis=1, keepdims=True))
        shrink = jnp.exp(old - new)
        expo = jnp.exp(scores - new[:, :1])
        top[spot, :] = new
        made = jnp.dot(expo.astype(BF16), vp[k_rows, :], preferred_element_type=F32)
        accum[spot, :128] = accum[spot, :128] * shrink + made[:, :128]
        accum[spot, 128:] = accum[spot, 128:] * shrink + made[:, 128:]

    def k_at(step):
        return pl.ds(pl.multiple_of(SLOTS + step * KEYS, 512), KEYS)

    def q_block(at, carry):
        begin = at * QROWS
        q_rows = pl.ds(pl.multiple_of(begin, QROWS), QROWS)
        top[...] = jnp.full_like(top, -1e29)
        accum[...] = jnp.zeros_like(accum)

        def both(k_rows, mask=None):
            size = k_rows.size
            first_scores[:, :size] = score(0, q_rows, k_rows)
            second_scores[:, :size] = score(1, q_rows, k_rows)
            absorb(0, first_scores[:, :size], k_rows, mask)
            absorb(1, second_scores[:, :size], k_rows, mask)

        def diagonal(size):
            row = begin + lax.broadcasted_iota(jnp.int32, (QROWS, size), 0)
            key = lax.broadcasted_iota(jnp.int32, (QROWS, size), 1)
            both(pl.ds(0, size), key < jnp.clip(row - mine + 1, 0, here))

        reached = begin + QROWS > mine
        pl.when(reached & (here <= SLOTS // 2))(lambda: diagonal(SLOTS // 2))
        pl.when(reached & (here > SLOTS // 2))(lambda: diagonal(SLOTS))

        @pl.when(k_half > 0)
        def _():
            both(pl.ds(pl.multiple_of(SLOTS + k_blocks * KEYS, 512), KEYS // 2))

        @pl.when(k_blocks > 0)
        def _():
            first_scores[...] = score(0, q_rows, k_at(0))

        def k_block(step, carry):
            second_scores[...] = score(1, q_rows, k_at(step))
            absorb(0, first_scores[...], k_at(step))
            first_scores[...] = score(0, q_rows, k_at(jnp.minimum(step + 1, k_blocks - 1)))
            absorb(1, second_scores[...], k_at(step))
            return carry

        lax.fori_loop(0, k_blocks, k_block, 0)
        spot = lax.broadcasted_iota(jnp.int32, (QROWS, 128), 1)
        kept = jnp.zeros((QROWS, 128), F32)
        for head in range(2):
            part = slice(head * QROWS, (head + 1) * QROWS)
            whole = accum[part, 128:129]
            op[q_rows, head * 128 : (head + 1) * 128] = (
                accum[part, :128] / jnp.maximum(whole, 1e-30)
            ).astype(BF16)
            kept = jnp.where(spot == 2 * head, top[part, :], kept)
            kept = jnp.where(spot == 2 * head + 1, whole, kept)
        sp[q_rows, :] = kept
        return carry

    lax.fori_loop(0, q_blocks, q_block, 0)
    for at in range(NX):
        rows = pl.ds(pl.multiple_of(q_from[at], 16), SLOTS)
        out[at] = op[rows, :]
        stats[at] = jnp.transpose(sp[rows, :])[:8]


def attend(query, pair):
    packed_q = (NX + 1) * SLOTS
    packed_k = (NZ + 1) * SLOTS + KEYS
    return pl.pallas_call(
        attend_kernel,
        out_shape=(
            jax.ShapeDtypeStruct((NX, SLOTS, 256), BF16),
            jax.ShapeDtypeStruct((NX, 8, SLOTS), F32),
        ),
        in_specs=[VMEM, VMEM],
        out_specs=(VMEM, VMEM),
        scratch_shapes=[
            pltpu.VMEM((packed_k, 256), BF16),
            pltpu.VMEM((packed_k, 256), BF16),
            pltpu.VMEM((2, packed_q, 256), BF16),
            pltpu.VMEM((packed_q, 256), BF16),
            pltpu.VMEM((packed_q, 128), F32),
            pltpu.VMEM((2 * QROWS, 128), F32),
            pltpu.VMEM((2 * QROWS, 256), F32),
            pltpu.VMEM((QROWS, KEYS), F32),
            pltpu.VMEM((QROWS, KEYS), F32),
            pltpu.VMEM((16, 128), jnp.int32),
            pltpu.SMEM((16, 128), jnp.int32),
            pltpu.SemaphoreType.DMA,
        ],
        compiler_params=pltpu.CompilerParams(vmem_limit_bytes=28 * MIB),
        cost_estimate=pl.CostEstimate(flops=4 << 30, bytes_accessed=8 << 20, transcendentals=4 << 20),
        name="attend",
    )(query, pair)


def merge_kernel(
    part_out, stats, gate, columns, update,
    came, came_stats, relay, own, held, weights, total,
    x_send, x_recv, s_send, s_recv, a_send, a_recv, local_sem,
):
    ctx, tp = lax.axis_index("ctx"), lax.axis_index("tp")
    z, x = ctx // NX, ctx % NX
    right, left, far = (x + 1) % NX, (x + NX - 1) % NX, (x + 2) % NX

    def at_x(at):
        return (z * NX + at, tp)

    spans = [(part * ROWS, ROWS) for part in range(MERGES)]
    gather = TpGather(own, held, (a_send, a_recv), spans)
    share = columns.shape[2]
    loads = [
        pltpu.make_async_copy(columns.at[at], weights.at[:, pl.ds(at * share, share)], local_sem.at[at])
        for at in range(NX)
    ]
    for load in loads:
        load.start()
    partners = gather.partners + [at_x(right), at_x(left), at_x(far)]
    greet(partners)
    await_greetings(partners)

    copies = {}

    def send(part, item, src, dst, device):
        copy = remote(src, dst, (x_send, x_recv), part * 6 + item, device)
        copy.start()
        copies[part, item] = copy

    told = []
    for item, to in enumerate((right, left, far)):
        copy = remote(stats.at[to], came_stats.at[x], (s_send, s_recv), item, at_x(to))
        copy.start()
        told.append(copy)

    def begin(part):
        rows = spans[part]
        low, high = halves(*rows)
        send(part, 2, part_out.at[far, pl.ds(*low)], relay.at[part, 0], at_x(right))
        send(part, 3, part_out.at[far, pl.ds(*high)], relay.at[part, 1], at_x(left))
        send(part, 0, part_out.at[right, pl.ds(*rows)], came.at[x, pl.ds(*rows)], at_x(right))
        send(part, 1, part_out.at[left, pl.ds(*rows)], came.at[x, pl.ds(*rows)], at_x(left))

    def middle(part):
        low, high = halves(*spans[part])
        copies[part, 2].wait_recv()
        send(part, 4, relay.at[part, 0], came.at[left, pl.ds(*low)], at_x(right))
        copies[part, 3].wait_recv()
        send(part, 5, relay.at[part, 1], came.at[right, pl.ds(*high)], at_x(left))

    def combine(part):
        for item in (0, 1, 4, 5):
            copies[part, item].wait_recv()
        lo = part * ROWS
        lines = [stats[x, :, lo : lo + ROWS]] + [
            came_stats[at, :, lo : lo + ROWS] for at in (right, left, far)
        ]
        shares = []
        for head in range(2):
            tops = [line[2 * head : 2 * head + 1] for line in lines]
            best = functools.reduce(jnp.maximum, tops)
            mass = [
                line[2 * head + 1 : 2 * head + 2] * jnp.exp(one - best)
                for line, one in zip(lines, tops)
            ]
            whole = jnp.maximum(sum(mass), 1e-30)
            shares += [one / whole for one in mass]
        turned = jnp.transpose(
            jnp.concatenate(shares + [jnp.zeros((120, ROWS), F32)], axis=0)
        )
        blocks = [part_out[x, lo : lo + ROWS, :]] + [
            came[at, lo : lo + ROWS, :] for at in (right, left, far)
        ]
        for head in range(2):
            mixed = sum(
                block[:, head * 128 : (head + 1) * 128].astype(F32)
                * turned[:, head * 4 + i : head * 4 + i + 1]
                for i, block in enumerate(blocks)
            ).astype(BF16)
            own[lo : lo + ROWS, head * 128 : (head + 1) * 128] = mixed
            held[tp, lo : lo + ROWS, head * 128 : (head + 1) * 128] = mixed

    def finish(lo):
        for part in range(lo // ROWS, (lo + DONE) // ROWS):
            gather.settle(part)
        total[...] = jnp.zeros_like(total)

        @pl.loop(0, TP)
        def _(slot):
            total[...] += jnp.dot(
                held[slot, lo : lo + DONE, :], weights[slot], preferred_element_type=F32
            )

        update[lo : lo + DONE, :] = (total[...] * gate[lo : lo + DONE, :1]).astype(BF16)

    def pass_on(part):
        combine(part)
        gather.begin(part)

    begin(0)
    middle(0)
    begin(1)
    for copy in told:
        copy.wait_recv()
    pass_on(0)
    middle(1)
    gather.middle(0)
    pass_on(1)
    gather.end(0)
    for load in loads:
        load.wait()
    gather.middle(1)
    finish(0)
    gather.end(1)
    finish(DONE)
    for copy in told + list(copies.values()):
        copy.wait_send()
    gather.drain()


def merge(part_out, stats, gate, columns):
    share, width = columns.shape[2:]
    dma = pltpu.SemaphoreType.DMA
    return pl.pallas_call(
        merge_kernel,
        out_shape=jax.ShapeDtypeStruct((SLOTS, width), BF16),
        in_specs=[VMEM, VMEM, VMEM, FAR],
        out_specs=VMEM,
        scratch_shapes=[
            pltpu.VMEM((NX, SLOTS, 256), BF16),
            pltpu.VMEM((NX, 8, SLOTS), F32),
            pltpu.VMEM((MERGES, 2, ROWS // 2, 256), BF16),
            pltpu.VMEM((SLOTS, 256), BF16),
            pltpu.VMEM((TP, SLOTS, 256), BF16),
            pltpu.VMEM((TP, NX * share, width), BF16),
            pltpu.VMEM((DONE, width), F32),
            dma((MERGES * 6,)), dma((MERGES * 6,)),
            dma((3,)), dma((3,)),
            dma((MERGES * 9,)), dma((MERGES * 9,)),
            dma((NX,)),
        ],
        compiler_params=pltpu.CompilerParams(
            collective_id=1, has_side_effects=True, vmem_limit_bytes=20 * MIB
        ),
        cost_estimate=pl.CostEstimate(flops=1 << 30, bytes_accessed=8 << 20, transcendentals=0),
        name="merge",
    )(part_out, stats, gate, columns)


WINDOW = 64


def spread_kernel(counts, tokens, rank, update, out, made, sems):
    blocks = rank.shape[0]
    turned = jnp.transpose(rank[...])
    slot = lax.broadcasted_iota(jnp.int32, (128, WINDOW), 1).astype(F32)
    before = jnp.int32(0)
    copies = []
    for b in range(blocks):
        first = jnp.minimum(before // 16 * 16, SLOTS - WINDOW)
        place = jnp.where(turned[:, b : b + 1] - first.astype(F32) == slot, 1.0, 0.0).astype(BF16)
        near = update[pl.ds(pl.multiple_of(first, 16), WINDOW), :]
        added = jnp.dot(place, near, preferred_element_type=F32)
        rows = slice(b * 128, (b + 1) * 128)
        made[rows, :] = (tokens[rows, :].astype(F32) + added).astype(BF16)
        before = before + counts[b]
        if b % 4 == 3:
            rows = pl.ds((b - 3) * 128, 512)
            copies.append(pltpu.make_async_copy(made.at[rows], out.at[rows], sems.at[b // 4]))
            copies[-1].start()
    for copy in copies:
        copy.wait()


def spread(counts, tokens, rank, update):
    return pl.pallas_call(
        spread_kernel,
        out_shape=jax.ShapeDtypeStruct(tokens.shape, BF16),
        in_specs=[pl.BlockSpec(memory_space=pltpu.SMEM), VMEM, VMEM, VMEM],
        out_specs=FAR,
        scratch_shapes=[
            pltpu.VMEM(tokens.shape, BF16),
            pltpu.SemaphoreType.DMA((rank.shape[0] // 4,)),
        ],
        compiler_params=pltpu.CompilerParams(vmem_limit_bytes=12 * MIB),
        cost_estimate=pl.CostEstimate(flops=1 << 28, bytes_accessed=5 << 20, transcendentals=0),
        name="spread",
    )(counts, tokens, rank, update)


def body(tokens, block_counts, block_orders, w_router, w_query, w_key, w_value, w_out):
    far = [
        pltpu.with_memory_space_constraint(array, pltpu.HBM)
        for array in (tokens, block_counts, block_orders, w_router, w_query, w_key, w_value, w_out)
    ]
    query, pair, gate, columns, rank = project(*far)
    part_out, stats = attend(query, pair)
    update = merge(part_out, stats, gate, columns)
    return spread(block_counts, tokens, rank, update)


def solution(mesh):
    return jax.shard_map(
        body,
        mesh=mesh,
        in_specs=(
            P("ctx", "tp"),
            P("ctx"),
            P("ctx", None),
            P("tp"),
            P(None, "tp"),
            P(None, "tp"),
            P(None, "tp"),
            P("tp", None),
        ),
        out_specs=P("ctx", "tp"),
        check_vma=False,
    )
```
